256 devices in a mesh: corpus: 32 (over x, y, core), qbatch: 8 (over z).
Axes of the slice: x: 4, y: 4, z: 8, core: 2. Of those that a mesh axis runs over, the one named last changes fastest.
Arguments:
- query_tokens: bfloat16 [4096, 32, 128], P(('corpus', 'qbatch')), may hold values from -6 to 6
- visit_owner: int32 [4096, 8], P(('corpus', 'qbatch')), may hold values from 0 to 255, as said below
- visit_passages: int32 [4096, 8, 8], P(('corpus', 'qbatch')), may hold values from 0 to 63
- passage_tokens: bfloat16 [16384, 128, 128], P(('corpus', 'qbatch')), may hold values from -0.015625 to 0.015625
- passage_lengths: int32 [16384], P(('corpus', 'qbatch')), may hold values from 16 to 128
Outputs:
- scores: float32 [4096, 64], P(('corpus', 'qbatch'))
The draws below stay inside these ranges and needn't reach their ends.
Inputs may be any that keep to these rules, and one draw needn't show every extreme that they name: `visit_owner`: the 8 owners of one query differ. The 128 queries of the devices that share a corpus index visit exactly half of the 256 owners, each of them exactly 8 times; some owners are visited so by every such group.
All inputs are finite; a program needn't handle non-finite values.
Results may differ from the reference program's by a relative error of at most 0.0003.
Values may be sent and summed in bfloat16 or wider, within the bound.
No kernel may reach another device: no remote copies, remote signals or barrier semaphores. Data moves between devices by JAX's collectives and lax.ppermute only.
A program may use at most 64 MiB of HBM per device.

```python
import jax
import jax.numpy as jnp
from jax import lax

D = 128
QTOK = 32
PTOK = 128
VISITS = 8
PER_VISIT = 8
P_DEV = 64
OWNERS = 256
GROUPS = 32
GROUP_Q = 128
QUERIES = 4096
PASSAGES = 16384


def draw_visit_owner(key, part):
    key = jax.random.fold_in(key, 11)
    hot_count = max(OWNERS // 16, 1)
    active_count = OWNERS // 2
    rank_of = jax.random.permutation(jax.random.fold_in(key, 1), OWNERS)
    is_hot = (rank_of < hot_count).astype(jnp.int32)
    random_keys = jax.random.randint(jax.random.fold_in(key, 2), (GROUPS, OWNERS), 0, 2 ** 20)
    owner_keys = (random_keys + (1 - is_hot)[None, :] * 2 ** 20) * OWNERS + jnp.arange(OWNERS, dtype=jnp.int32)[None, :]
    chosen = jnp.argsort(owner_keys, axis=1)[:, :active_count]
    positions = jnp.arange(GROUP_Q * VISITS, dtype=jnp.int32) % active_count
    owners = chosen[:, positions].reshape(GROUPS, GROUP_Q, VISITS)

    def shuffle_rows(sub_key):
        return jax.random.permutation(sub_key, GROUP_Q)
    shuffles = jax.vmap(shuffle_rows)(jax.random.split(jax.random.fold_in(key, 3), GROUPS))
    owners = jnp.take_along_axis(owners, shuffles[:, :, None], axis=1)
    return owners.reshape(QUERIES, VISITS).astype(jnp.int32)


def set_ends(values, stream_key, smallest, largest):
    dims = values.shape
    place = [jax.random.randint(jax.random.fold_in(stream_key, axis), (), 0, dims[axis]) for axis in range(len(dims))]
    values = values.at[tuple(place)].set(smallest)
    longest = dims.index(max(dims))
    place[longest] = (place[longest] + 1) % dims[longest]
    return values.at[tuple(place)].set(largest)


def level_of(own_key, shape, cuts, least, largest):
    level, own = 1.0, jax.random.fold_in(own_key, 6)
    for position, shards_of in cuts:
        steps = jnp.exp(jax.random.uniform(jax.random.fold_in(own, position), (shards_of,), jnp.float32, least / len(cuts), largest / len(cuts)))
        level = level * jnp.repeat(steps, shape[position] // shards_of).reshape([-1 if axis == position else 1 for axis in range(len(shape))])
    return level


def normal_values(key, extent, deviation, bound, cuts=(), kind=jnp.bfloat16):
    entries = deviation * jax.random.normal(key, extent, jnp.float32)
    if cuts:
        entries = entries * level_of(key, extent, cuts, -0.22, 0.18)
    return jnp.clip(entries, -bound, bound).astype(kind)


def setup_inputs(seed: int = 0) -> dict:
    arg_keys = jax.random.split(jax.random.key(seed), 6)
    query_tokens = normal_values(arg_keys[0], (QUERIES, QTOK, D), 1.0, 6.0, ((0, 256),))
    visit_owner = draw_visit_owner(jax.random.fold_in(arg_keys[5], 71), 0)
    visit_passages = set_ends(jax.random.randint(arg_keys[2], (QUERIES, VISITS, PER_VISIT), 0, P_DEV), jax.random.fold_in(arg_keys[2], 1), 0, P_DEV - 1).astype(jnp.int32)
    passage_tokens = normal_values(arg_keys[3], (PASSAGES, PTOK, D), (D * QTOK * QTOK) ** -0.5, 0.015625, ((0, 256),))
    passage_lengths = set_ends(jax.random.randint(arg_keys[4], (PASSAGES,), PTOK // 8, PTOK + 1), jax.random.fold_in(arg_keys[4], 1), PTOK // 8, PTOK).astype(jnp.int32)
    return dict(query_tokens=query_tokens, visit_owner=visit_owner, visit_passages=visit_passages, passage_tokens=passage_tokens, passage_lengths=passage_lengths)


def reference(query_tokens, visit_owner, visit_passages, passage_tokens, passage_lengths):
    global_cands = (visit_owner[:, :, None] * P_DEV + visit_passages).astype(jnp.int32)
    global_cands = global_cands.reshape(QUERIES, VISITS * PER_VISIT)
    token_index = jnp.arange(PTOK, dtype=jnp.int32)

    def one_query(pieces):
        query_rows, cand_rows = pieces
        passages = passage_tokens[cand_rows].astype(jnp.float32)
        similarity = jnp.einsum("id,cjd->cij", query_rows.astype(jnp.float32), passages, precision=lax.Precision.HIGHEST)
        in_length = token_index[None, None, :] < passage_lengths[cand_rows][:, None, None]
        best_match = jnp.max(jnp.where(in_length, similarity, -1e30), axis=2)
        return jnp.sum(best_match, axis=1)

    return lax.map(one_query, (query_tokens, global_cands))
```

```python
import jax
import jax.numpy as jnp
from jax import lax
from jax.experimental import pallas as pl
from jax.experimental.pallas import tpu as pltpu
from jax.sharding import PartitionSpec as P

f32, bf16, i32 = jnp.float32, jnp.bfloat16, jnp.int32
TOK = 32
FEAT = 128
PLEN = 128
LOCAL = 64
VIS = 8
QDEV = 16
ROWS = 8
COLS = 32
GROUP = QDEV * ROWS
SLOTS = COLS * VIS
BLOCK = QDEV * TOK + QDEV
CELL = VIS * TOK + QDEV
TILE = 8
UNROLL = 8
PLANES = SLOTS // TILE + UNROLL
VMEM_LIMIT = 48 * 1024 * 1024


def iota(shape, dim):
    return lax.broadcasted_iota(i32, shape, dim)


def dot_t(a, b, precision=None):
    return lax.dot_general(
        a, b, (((1,), (1,)), ((), ())), precision=precision, preferred_element_type=f32
    )


def dot_n(a, b, precision=None):
    return lax.dot_general(
        a, b, (((1,), (0,)), ((), ())), precision=precision, preferred_element_type=f32
    )


def fill_kernel(length_ref, tokens_ref, out_ref):
    token = iota((PLEN, FEAT), 0)

    def one(p, _):
        tokens = tokens_ref[p].astype(f32)
        out_ref[p] = jnp.where(token < length_ref[p], tokens, tokens[0:1, :]).astype(bf16)
        return 0

    lax.fori_loop(0, LOCAL, one, 0)


def build_kernel(row_ref, *refs):
    blocks = refs[:ROWS]
    send_ref, back_ref, buf, idx_v, idx_s, sems, idx_sem = refs[ROWS:]
    row = row_ref[0]
    copies = []
    for s, (block, step) in enumerate(zip(blocks, STEPS)):
        copy = pltpu.make_async_copy(block, buf.at[lax.rem(row + step, ROWS)], sems.at[s])
        copy.start()
        copies.append(copy)
    for copy in copies:
        copy.wait()
    lists = jnp.concatenate([buf[z, QDEV * TOK : BLOCK, :] for z in range(ROWS)], 0)
    eye = (iota((GROUP, FEAT), 0) == iota((GROUP, FEAT), 1)).astype(bf16)
    owners = dot_t(eye[0:QDEV], lists)
    wanted = (iota((COLS, GROUP), 0) * ROWS + (row + 1)).astype(f32)
    hit = jnp.zeros((COLS, GROUP), f32)
    for v in range(VIS):
        hit = jnp.where(owners[v : v + 1, :] == wanted, 1.0, hit)
    before = (iota((GROUP, GROUP), 0) < iota((GROUP, GROUP), 1)).astype(bf16)
    rank = dot_n(hit.astype(bf16), before)
    rank = jnp.where(hit > 0.5, rank, -1.0)
    place = iota((COLS, QDEV, GROUP), 1).astype(f32)
    pick = jnp.where(rank[:, None, :] == place, 1.0, 0.0)
    chosen = pick.reshape(COLS * QDEV, GROUP).astype(bf16)
    number = iota((QDEV, GROUP), 1).astype(bf16)
    idx_v[...] = dot_t(number, chosen)[0:8, :].astype(i32)
    to_scalar = pltpu.make_async_copy(idx_v, idx_s, idx_sem)
    to_scalar.start()
    send_ref[:, VIS * TOK : CELL, :] = (
        dot_n(chosen, lists).astype(bf16).reshape(COLS, QDEV, FEAT)
    )
    slots = pick[:, 0:VIS, :].reshape(SLOTS, GROUP).astype(bf16)
    back_ref[...] = dot_t(eye, slots)
    to_scalar.wait()

    def one(c, _):
        for s in range(VIS):
            q = idx_s[0, c * QDEV + s]
            start = pl.multiple_of((q & (QDEV - 1)) * TOK, TOK)
            send_ref[c, s * TOK : (s + 1) * TOK, :] = buf[q >> 4, pl.ds(start, TOK), :]
        return 0

    lax.fori_loop(0, COLS, one, 0)


def score_kernel(me_ref, got_ref, lists_ref, passage_ref, out_ref, plan_v, plan_s, best, plan_sem):
    me = me_ref[0].astype(f32)
    lists = lists_ref[...].astype(f32)[:, 0:VIS, :].reshape(SLOTS, FEAT)
    lane = iota((SLOTS, FEAT), 1)
    visit = jnp.where((lists == me) & (lane < VIS), 1.0, 0.0).astype(bf16)
    low, high = iota((FEAT, FEAT), 0), iota((FEAT, FEAT), 1)
    spread = ((high >= VIS) & (low == (high >> 3) - 1)).astype(bf16)
    mine = dot_n(visit, spread)
    kept = (lists * mine).astype(bf16)
    k16, l16 = iota((16, FEAT), 0), iota((16, FEAT), 1)
    fold = ((l16 >= VIS) & (l16 < VIS + VIS * VIS) & ((l16 & 7) == k16)).astype(bf16)
    cands = dot_t(fold, kept)

    wide = (LOCAL, SLOTS)
    passage = (iota(wide, 0) + 1).astype(f32)
    slot = iota(wide, 1)
    hit = jnp.zeros(wide, f32)
    for k in range(VIS):
        hit = jnp.where(cands[k : k + 1, :] == passage, 1.0, hit)
    before = (iota((SLOTS, SLOTS), 0) < iota((SLOTS, SLOTS), 1)).astype(bf16)
    rank = dot_n(hit.astype(bf16), before).astype(i32)
    count = jnp.sum(hit, axis=1, keepdims=True).astype(i32)
    tiles = (count + (TILE - 1)) >> 3
    tiles_wide = jnp.broadcast_to(tiles, (LOCAL, FEAT)).astype(f32)
    earlier = (iota((LOCAL, LOCAL), 1) < iota((LOCAL, LOCAL), 0)).astype(bf16)
    first = dot_n(earlier, tiles_wide.astype(bf16))[:, 0:1].astype(i32)
    total = jnp.sum(tiles_wide[:, 0:1], axis=0, keepdims=True).astype(i32)
    deepest = jnp.max(tiles_wide[:, 0:1], axis=0, keepdims=True).astype(i32)

    shift = slot - rank
    start = slot * 2 + (slot >> 3)
    x = jnp.where(hit > 0.5, shift * 1024 + start + 1, 0)
    for b in range(8):
        moves = ((x >> (10 + b)) & 1) == 1
        x = jnp.where(moves, 0, x) + pltpu.roll(jnp.where(moves, x, 0), SLOTS - (1 << b), 1)
    plan_v[0:LOCAL, :] = jnp.maximum((x & 1023) - 1, 0)
    for half in range(2):
        t = slot + half * SLOTS
        begun = first <= t
        which = jnp.sum(jnp.where(begun, 1.0, 0.0), axis=0, keepdims=True).astype(i32) - 1
        since = jnp.max(jnp.where(begun, first, 0).astype(f32), axis=0, keepdims=True).astype(i32)
        plan_v[LOCAL + half : LOCAL + half + 1, :] = which * 64 + jnp.minimum(t[0:1, :] - since, 63)
    plan_v[LOCAL + 2 : LOCAL + 3, :] = jnp.broadcast_to(total, (1, SLOTS))
    plan_v[LOCAL + 3 : LOCAL + 4, :] = jnp.broadcast_to(deepest, (1, SLOTS))
    to_scalar = pltpu.make_async_copy(plan_v, plan_s, plan_sem)
    to_scalar.start()
    to_scalar.wait()

    def tile_steps(step, _):
        for u in range(UNROLL):
            t = step * UNROLL + u
            word = plan_s[LOCAL + (step >> 5), t & (SLOTS - 1)]
            p = word >> 6
            j = word & 63
            base = jnp.minimum(j, SLOTS // TILE - 1) * TILE
            queries = jnp.concatenate(
                [
                    got_ref[pl.ds(pl.multiple_of(plan_s[p, base + r] * 16, 16), TOK), :]
                    for r in range(TILE)
                ],
                0,
            )
            similarity = dot_t(passage_ref[p], queries)
            best[j, pl.ds(p, 1), :] = jnp.max(similarity, axis=0, keepdims=True)
        return 0

    steps = (plan_s[LOCAL + 2, 0] + (UNROLL - 1)) >> 3
    lax.fori_loop(0, steps, tile_steps, 0)

    adder = ((iota((SLOTS, FEAT), 0) >> 5) == (iota((SLOTS, FEAT), 1) & 7)).astype(f32)

    def gather_plane(j, acc):
        sums = dot_n(best[j], adder, lax.Precision.HIGHEST)
        both = jnp.concatenate([sums, sums], 1)
        return jnp.where((slot >> 3) == j, both, acc)

    y = lax.fori_loop(0, plan_s[LOCAL + 3, 0], gather_plane, jnp.zeros(wide, f32))
    y = jnp.where(slot < count, y, 0.0)
    x = x >> 10
    for b in (7, 6, 5, 4, 3, 2, 1, 0):
        moves = ((x >> b) & 1) == 1
        y = jnp.where(moves, 0.0, y) + pltpu.roll(jnp.where(moves, y, 0.0), 1 << b, 1)
        x = jnp.where(moves, 0, x) + pltpu.roll(jnp.where(moves, x, 0), 1 << b, 1)
    scores = jnp.concatenate(
        [
            jnp.sum(jnp.where(cands[k : k + 1, :] == passage, y, 0.0), axis=0, keepdims=True)
            for k in range(VIS)
        ],
        0,
    )
    k8, l8 = iota((VIS, FEAT), 0), iota((VIS, FEAT), 1)
    repeat = ((l8 & 7) == k8).astype(f32)
    spread_back = ((high < VIS * VIS) & (low == (high >> 3))).astype(bf16)
    by_slot = lax.dot_general(
        scores,
        repeat,
        (((0,), (0,)), ((), ())),
        precision=lax.Precision.HIGHEST,
        preferred_element_type=f32,
    )
    out_ref[...] = by_slot * dot_n(visit, spread_back)


def return_kernel(back_ref, got_ref, out_ref):
    out_ref[...] = dot_n(back_ref[...], got_ref[...], lax.Precision.HIGHEST)


VM = pl.BlockSpec(memory_space=pltpu.VMEM)
SM = pl.BlockSpec(memory_space=pltpu.SMEM)
ANY = pl.BlockSpec(memory_space=pl.ANY)
PARAMS = pltpu.CompilerParams(vmem_limit_bytes=VMEM_LIMIT)
STEPS = (0, 7, 1, 6, 2, 5, 3, 4)


def fill(lengths, tokens):
    return pl.pallas_call(
        fill_kernel,
        out_shape=jax.ShapeDtypeStruct((LOCAL, PLEN, FEAT), bf16),
        in_specs=[SM, VM],
        out_specs=VM,
        compiler_params=PARAMS,
        cost_estimate=pl.CostEstimate(flops=1 << 22, bytes_accessed=1 << 22, transcendentals=0),
    )(lengths, tokens)


def build(row, blocks):
    return pl.pallas_call(
        build_kernel,
        out_shape=(
            jax.ShapeDtypeStruct((COLS, CELL, FEAT), bf16),
            jax.ShapeDtypeStruct((GROUP, SLOTS), f32),
        ),
        in_specs=[SM] + [ANY] * ROWS,
        out_specs=(VM, VM),
        scratch_shapes=[
            pltpu.VMEM((ROWS, BLOCK, FEAT), bf16),
            pltpu.VMEM((8, COLS * QDEV), i32),
            pltpu.SMEM((8, COLS * QDEV), i32),
            pltpu.SemaphoreType.DMA((ROWS,)),
            pltpu.SemaphoreType.DMA,
        ],
        compiler_params=PARAMS,
    )(row, *blocks)


def score(me, got, passages):
    lists = got[:, VIS * TOK : CELL, :]
    return pl.pallas_call(
        score_kernel,
        out_shape=jax.ShapeDtypeStruct((SLOTS, FEAT), f32),
        in_specs=[SM, VM, VM, VM],
        out_specs=VM,
        scratch_shapes=[
            pltpu.VMEM((LOCAL + 8, SLOTS), i32),
            pltpu.SMEM((LOCAL + 8, SLOTS), i32),
            pltpu.VMEM((PLANES, LOCAL, SLOTS), f32),
            pltpu.SemaphoreType.DMA,
        ],
        compiler_params=PARAMS,
    )(me, got.reshape(COLS * CELL, FEAT), lists, passages)


def hand_back(back, got):
    return pl.pallas_call(
        return_kernel,
        out_shape=jax.ShapeDtypeStruct((GROUP, FEAT), f32),
        in_specs=[VM, VM],
        out_specs=VM,
        compiler_params=PARAMS,
    )(back, got)


def shards(query_tokens, visit_owner, visit_passages, passage_tokens, passage_lengths):
    row = lax.axis_index("qbatch").astype(i32)
    me = lax.axis_index("corpus").astype(i32) * ROWS + row + 1
    lists = jnp.concatenate(
        [
            visit_owner + 1,
            visit_passages.reshape(QDEV, VIS * VIS) + 1,
            jnp.zeros((QDEV, FEAT - VIS - VIS * VIS), i32),
        ],
        1,
    ).astype(bf16)
    own = jnp.concatenate([query_tokens.reshape(QDEV * TOK, FEAT), lists], 0)
    up = [(i, (i + 1) % ROWS) for i in range(ROWS)]
    down = [(i, (i + ROWS - 1) % ROWS) for i in range(ROWS)]
    blocks = [own]
    left = right = own
    for step in range(1, ROWS // 2 + 1):
        left = lax.ppermute(left, "qbatch", up)
        blocks.append(left)
        if step < ROWS // 2:
            right = lax.ppermute(right, "qbatch", down)
            blocks.append(right)
    passages = fill(passage_lengths, passage_tokens)
    send, back = build(row[None], blocks)
    got = lax.all_to_all(send, "corpus", split_axis=0, concat_axis=0, tiled=True)
    scored = score(me[None], got, passages)
    returned = lax.all_to_all(
        scored.reshape(COLS, VIS, FEAT), "corpus", split_axis=0, concat_axis=0, tiled=True
    )
    mine = hand_back(back, returned.reshape(SLOTS, FEAT))
    parts = lax.all_to_all(
        mine.reshape(ROWS, QDEV, FEAT), "qbatch", split_axis=0, concat_axis=0, tiled=True
    )
    return jnp.sum(parts, axis=0)[:, 0 : VIS * VIS]


def solution(mesh):
    placed = (
        P(("corpus", "qbatch"), None, None),
        P(("corpus", "qbatch"), None),
        P(("corpus", "qbatch"), None, None),
        P(("corpus", "qbatch"), None, None),
        P(("corpus", "qbatch")),
    )
    return jax.shard_map(
        shards, mesh=mesh, in_specs=placed, out_specs=P(("corpus", "qbatch"), None), check_vma=False
    )
```

```python
import jax
import jax.numpy as jnp
from jax import lax
from jax.experimental import pallas as pl
from jax.experimental.pallas import tpu as pltpu
from jax.sharding import PartitionSpec as P

f32, bf16, i32 = jnp.float32, jnp.bfloat16, jnp.int32
TOK = 32
FEAT = 128
PLEN = 128
LOCAL = 64
VIS = 8
QDEV = 16
ROWS = 8
COLS = 32
GROUP = QDEV * ROWS
SLOTS = COLS * VIS
PIECES = TOK + 1
CELL = VIS * 2 + 1
TILE = 8
TILES = 384
UNROLL = 16
PARTS = ((0, 8), (8, 16), (16, 24), (24, 30), (30, 32))
VMEM_LIMIT = 16 * 1024 * 1024


def iota(shape, dim):
    return lax.broadcasted_iota(i32, shape, dim)


def dot_t(a, b, precision=None):
    return lax.dot_general(
        a, b, (((1,), (1,)), ((), ())), precision=precision, preferred_element_type=f32
    )


def dot_n(a, b, precision=None):
    return lax.dot_general(
        a, b, (((1,), (0,)), ((), ())), precision=precision, preferred_element_type=f32
    )


def dot_tn(a, b, precision=None):
    return lax.dot_general(
        a, b, (((0,), (0,)), ((), ())), precision=precision, preferred_element_type=f32
    )


def fill_kernel(length_ref, tokens_ref, out_ref, filled, sem):
    token = iota((PLEN, FEAT), 0)

    def one(p, _):
        tokens = tokens_ref[p].astype(f32)
        filled[p] = jnp.where(token < length_ref[p], tokens, tokens[0:1, :]).astype(bf16)
        return 0

    lax.fori_loop(0, LOCAL, one, 0)
    copy = pltpu.make_async_copy(filled, out_ref, sem)
    copy.start()
    copy.wait()


def pack_kernel(tokens_ref, owner_ref, cand_ref, out_ref, owners, cands, sems):
    loads = [
        pltpu.make_async_copy(owner_ref, owners, sems.at[0]),
        pltpu.make_async_copy(cand_ref, cands, sems.at[1]),
        pltpu.make_async_copy(tokens_ref, out_ref.at[pl.ds(0, TOK)], sems.at[2]),
    ]
    for load in loads:
        load.start()
    loads[0].wait()
    loads[1].wait()
    rest = jnp.zeros((FEAT - VIS - VIS * VIS, QDEV), i32)
    lists = jnp.concatenate([owners[...] + 1, cands[...] + 1, rest], 0).astype(bf16)
    eye = (iota((FEAT, FEAT), 0) == iota((FEAT, FEAT), 1)).astype(bf16)
    out_ref[TOK] = dot_tn(lists, eye).astype(bf16)
    loads[2].wait()


def build_kernel(row_ref, *refs):
    blocks = refs[:ROWS]
    send_ref, back_ref, buf, out_v, idx_v, idx_s, sems, idx_sem, out_sems = refs[ROWS:]
    row = row_ref[0]
    copies = []
    for s, (block, step) in enumerate(zip(blocks, STEPS)):
        at = buf.at[pl.ds(lax.rem(row + step, ROWS) * PIECES, PIECES)]
        copy = pltpu.make_async_copy(block, at, sems.at[s])
        copy.start()
        copies.append(copy)
    for copy in copies:
        copy.wait()
    lists = jnp.concatenate([buf[z * PIECES + TOK] for z in range(ROWS)], 0)
    eye = (iota((GROUP, FEAT), 0) == iota((GROUP, FEAT), 1)).astype(bf16)
    owners = dot_t(eye[0:QDEV], lists)
    wanted = (iota((COLS, GROUP), 0) * ROWS + (row + 1)).astype(f32)
    hit = jnp.zeros((COLS, GROUP), f32)
    for v in range(VIS):
        hit = jnp.where(owners[v : v + 1, :] == wanted, 1.0, hit)
    before = (iota((GROUP, GROUP), 0) < iota((GROUP, GROUP), 1)).astype(bf16)
    rank = dot_n(hit.astype(bf16), before)
    rank = jnp.where(hit > 0.5, rank, -1.0)
    place = iota((COLS, QDEV, GROUP), 1).astype(f32)
    pick = jnp.where(rank[:, None, :] == place, 1.0, 0.0)
    chosen = pick.reshape(COLS * QDEV, GROUP).astype(bf16)
    number = iota((QDEV, GROUP), 1).astype(bf16)
    query = dot_t(number, chosen)[0:8, :].astype(i32)
    idx_v[...] = (query >> 4) * PIECES + (query & (QDEV - 1)) * 2
    to_scalar = pltpu.make_async_copy(idx_v, idx_s, idx_sem)
    to_scalar.start()
    out_v[:, VIS * 2] = dot_n(chosen, lists).astype(bf16).reshape(COLS, QDEV, FEAT)
    slots = pick[:, 0:VIS, :].reshape(SLOTS, GROUP).astype(bf16)
    back_ref[...] = dot_t(eye, slots)
    to_scalar.wait()

    def one(c, _):
        for s in range(VIS):
            out_v[c, 2 * s : 2 * s + 2] = buf[pl.ds(idx_s[0, c * QDEV + s], 2)]
        return 0

    outs = []
    for start, stop in PARTS:
        lax.fori_loop(start, stop, one, 0)
        some = pl.ds(start, stop - start)
        copy = pltpu.make_async_copy(out_v.at[some], send_ref.at[some], out_sems.at[len(outs)])
        copy.start()
        outs.append(copy)
    for copy in outs:
        copy.wait()


def split3(x):
    high = x.astype(bf16)
    x = x - high.astype(f32)
    mid = x.astype(bf16)
    return high, mid, (x - mid.astype(f32)).astype(bf16)


def score_kernel(
    me_ref, got, cells_ref, passage_ref, out_ref, held, plan_v, plan_s, best, sems
):
    load = pltpu.make_async_copy(passage_ref, held, sems.at[0])
    load.start()
    me = me_ref[0].astype(f32)
    lists = cells_ref[:, VIS * 2].astype(f32)[:, 0:VIS, :].reshape(SLOTS, FEAT)
    lane = iota((SLOTS, FEAT), 1)
    visit = jnp.where((lists == me) & (lane < VIS), 1.0, 0.0).astype(bf16)
    low, high = iota((FEAT, FEAT), 0), iota((FEAT, FEAT), 1)
    spread = ((high >= VIS) & (low == (high >> 3) - 1)).astype(bf16)
    mine = dot_n(visit, spread)
    kept = (lists * mine).astype(bf16)
    k16, l16 = iota((16, FEAT), 0), iota((16, FEAT), 1)
    fold = ((l16 >= VIS) & (l16 < VIS + VIS * VIS) & ((l16 & 7) == k16)).astype(bf16)
    cands = dot_t(fold, kept)

    wide = (LOCAL, SLOTS)
    passage = (iota(wide, 0) + 1).astype(f32)
    slot = iota(wide, 1)
    hit = jnp.zeros(wide, f32)
    for k in range(VIS):
        hit = jnp.where(cands[k : k + 1, :] == passage, 1.0, hit)
    hits = hit.astype(bf16)
    before = (iota((SLOTS, SLOTS), 0) < iota((SLOTS, SLOTS), 1)).astype(bf16)
    rank = dot_n(hits, before).astype(i32)
    count = jnp.sum(hit, axis=1, keepdims=True).astype(i32)
    tiles = (count + (TILE - 1)) >> 3
    tiles_wide = jnp.broadcast_to(tiles, (LOCAL, FEAT)).astype(bf16)
    earlier = (iota((LOCAL, LOCAL), 1) < iota((LOCAL, LOCAL), 0)).astype(bf16)
    first_wide = dot_n(earlier, tiles_wide).astype(i32)
    padded = jnp.concatenate([hits, jnp.zeros(wide, bf16)], 0)
    tiles_row = (dot_t(jnp.ones((16, SLOTS), bf16), padded).astype(i32) + (TILE - 1)) >> 3
    first_row = dot_n(tiles_row.astype(bf16), (low < high).astype(bf16)).astype(i32)
    total = first_row[0:1, FEAT - 1 : FEAT]

    shift = slot - rank
    x = jnp.where(hit > 0.5, shift * 512 + slot + 1, 0)
    for b in range(8):
        moves = ((x >> (9 + b)) & 1) == 1
        x = jnp.where(moves, 0, x) + pltpu.roll(jnp.where(moves, x, 0), SLOTS - (1 << b), 1)
    packed = jnp.maximum((x & 511) - 1, 0).astype(f32).astype(bf16)

    t = iota((TILES, FEAT), 0)
    own = (first_row[0:1] <= t) & (t < first_row[0:1] + tiles_row[0:1])
    own = jnp.where(own, 1.0, 0.0).astype(bf16)
    table = jnp.concatenate(
        [packed, (first_wide >> 4).astype(bf16), (first_wide & 15).astype(bf16)], 1
    )
    rows = dot_n(own[:, 0:LOCAL], table)
    begun = rows[:, SLOTS : SLOTS + FEAT].astype(i32) * 16
    depth = t - begun - rows[:, SLOTS + FEAT :].astype(i32)
    depth = jnp.concatenate([depth, depth], 1)
    here = ((iota((TILES, SLOTS), 1) >> 3) == depth) & (iota((TILES, SLOTS), 0) < total)
    chosen = jnp.where(here, rows[:, 0:SLOTS], 0.0).astype(bf16)
    k16, l16 = iota((16, SLOTS + FEAT), 0), iota((16, SLOTS + FEAT), 1)
    fold = jnp.where((l16 < SLOTS) & ((l16 & 7) == k16), 1.0, 0.0)
    fold = jnp.where((l16 >= SLOTS) & (k16 == TILE), (l16 - SLOTS).astype(f32), fold)
    plan = dot_t(fold.astype(bf16), jnp.concatenate([chosen, own], 1)).astype(i32)
    plan_v[0:TILE, :] = plan[0:TILE] * 2 + (plan[0:TILE] >> 3)
    plan_v[TILE : TILE + 1, :] = plan[TILE : TILE + 1]
    plan_v[TILE + 1 : TILE + 2, :] = jnp.broadcast_to(total, (1, TILES))
    to_scalar = pltpu.make_async_copy(plan_v, plan_s, sems.at[1])
    to_scalar.start()
    to_scalar.wait()
    load.wait()

    def tile_steps(step, _):
        for half in range(UNROLL // 8):
            found = []
            for u in range(8):
                t = step * UNROLL + half * 8 + u
                queries = jnp.concatenate(
                    [got[pl.ds(plan_s[r, t], 2)].reshape(TOK, FEAT) for r in range(TILE)], 0
                )
                similarity = dot_t(held[plan_s[TILE, t]], queries)
                found.append(jnp.max(similarity, axis=0, keepdims=True))
            at = pl.multiple_of(step * UNROLL + half * 8, 8)
            best[pl.ds(at, 8), :] = jnp.concatenate(found, 0)
        return 0

    lax.fori_loop(0, (plan_s[TILE + 1, 0] + (UNROLL - 1)) // UNROLL, tile_steps, 0)

    adder = ((iota((SLOTS, FEAT), 0) >> 5) == (iota((SLOTS, FEAT), 1) & 7)).astype(bf16)
    sums = dot_n(jnp.concatenate(split3(best[...]), 1), jnp.concatenate([adder] * 3, 0))
    sums = jnp.where(here, jnp.concatenate([sums, sums], 1), 0.0)
    first = first_wide[:, 0:1]
    t = iota((LOCAL, TILES), 1)
    owned = jnp.where((first <= t) & (t < first + tiles), 1.0, 0.0).astype(bf16)
    y = dot_n(jnp.concatenate([owned] * 3, 1), jnp.concatenate(split3(sums), 0))
    y = jnp.where(slot < count, y, 0.0)
    x = x >> 9
    for b in (7, 6, 5, 4, 3, 2, 1, 0):
        moves = ((x >> b) & 1) == 1
        y = jnp.where(moves, 0.0, y) + pltpu.roll(jnp.where(moves, y, 0.0), 1 << b, 1)
        x = jnp.where(moves, 0, x) + pltpu.roll(jnp.where(moves, x, 0), 1 << b, 1)
    scores = jnp.concatenate(
        [
            jnp.sum(jnp.where(cands[k : k + 1, :] == passage, y, 0.0), axis=0, keepdims=True)
            for k in range(VIS)
        ],
        0,
    )
    k8, l8 = iota((VIS, FEAT), 0), iota((VIS, FEAT), 1)
    repeat = ((l8 & 7) == k8).astype(f32)
    spread_back = ((high < VIS * VIS) & (low == (high >> 3))).astype(bf16)
    by_slot = dot_tn(scores, repeat, lax.Precision.HIGHEST)
    out_ref[...] = by_slot * dot_n(visit, spread_back)


def return_kernel(back_ref, got_ref, out_ref):
    out_ref[...] = dot_n(back_ref[...], got_ref[...], lax.Precision.HIGHEST)


VM = pl.BlockSpec(memory_space=pltpu.VMEM)
SM = pl.BlockSpec(memory_space=pltpu.SMEM)
ANY = pl.BlockSpec(memory_space=pl.ANY)
PARAMS = pltpu.CompilerParams(vmem_limit_bytes=VMEM_LIMIT)
STEPS = (0, 7, 1, 6, 2, 5, 3, 4)


def in_hbm(x):
    return pltpu.with_memory_space_constraint(x, pltpu.HBM)


def fill(lengths, tokens):
    return pl.pallas_call(
        fill_kernel,
        out_shape=pltpu.HBM((LOCAL, PLEN, FEAT), bf16),
        in_specs=[SM, VM],
        out_specs=ANY,
        scratch_shapes=[pltpu.VMEM((LOCAL, PLEN, FEAT), bf16), pltpu.SemaphoreType.DMA],
        compiler_params=PARAMS,
        cost_estimate=pl.CostEstimate(flops=1 << 22, bytes_accessed=1 << 22, transcendentals=0),
    )(lengths, tokens)


def pack(tokens, owners, cands):
    return pl.pallas_call(
        pack_kernel,
        out_shape=jax.ShapeDtypeStruct((PIECES, 16, FEAT), bf16),
        in_specs=[ANY, ANY, ANY],
        out_specs=VM,
        scratch_shapes=[
            pltpu.VMEM((VIS, QDEV), i32),
            pltpu.VMEM((VIS * VIS, QDEV), i32),
            pltpu.SemaphoreType.DMA((3,)),
        ],
        compiler_params=PARAMS,
    )(in_hbm(tokens), in_hbm(owners), in_hbm(cands))


def build(row, blocks):
    return pl.pallas_call(
        build_kernel,
        out_shape=(
            pltpu.HBM((COLS, CELL, 16, FEAT), bf16),
            jax.ShapeDtypeStruct((GROUP, SLOTS), f32),
        ),
        in_specs=[SM] + [ANY] * ROWS,
        out_specs=(ANY, VM),
        scratch_shapes=[
            pltpu.VMEM((ROWS * PIECES, 16, FEAT), bf16),
            pltpu.VMEM((COLS, CELL, 16, FEAT), bf16),
            pltpu.VMEM((8, COLS * QDEV), i32),
            pltpu.SMEM((8, COLS * QDEV), i32),
            pltpu.SemaphoreType.DMA((ROWS,)),
            pltpu.SemaphoreType.DMA,
            pltpu.SemaphoreType.DMA((len(PARTS),)),
        ],
        compiler_params=PARAMS,
    )(row, *blocks)


def score(me, got, passages):
    return pl.pallas_call(
        score_kernel,
        out_shape=jax.ShapeDtypeStruct((SLOTS, FEAT), f32),
        in_specs=[SM, VM, VM, ANY],
        out_specs=VM,
        scratch_shapes=[
            pltpu.VMEM((LOCAL, PLEN, FEAT), bf16),
            pltpu.VMEM((16, TILES), i32),
            pltpu.SMEM((16, TILES), i32),
            pltpu.VMEM((TILES, SLOTS), f32),
            pltpu.SemaphoreType.DMA((2,)),
        ],
        compiler_params=PARAMS,
    )(me, got.reshape(COLS * CELL, 16, FEAT), got, in_hbm(passages))


def hand_back(back, got):
    return pl.pallas_call(
        return_kernel,
        out_shape=jax.ShapeDtypeStruct((GROUP, FEAT), f32),
        in_specs=[VM, VM],
        out_specs=VM,
        compiler_params=PARAMS,
    )(back, got)


def shards(query_tokens, visit_owner, visit_passages, passage_tokens, passage_lengths):
    row = lax.axis_index("qbatch").astype(i32)
    me = lax.axis_index("corpus").astype(i32) * ROWS + row + 1
    own = pack(
        query_tokens.reshape(TOK, 16, FEAT),
        visit_owner.T,
        jnp.transpose(visit_passages, (1, 2, 0)).reshape(VIS * VIS, QDEV),
    )
    up = [(i, (i + 1) % ROWS) for i in range(ROWS)]
    down = [(i, (i + ROWS - 1) % ROWS) for i in range(ROWS)]
    blocks = [own]
    left = right = own
    for step in range(1, ROWS // 2 + 1):
        left = lax.ppermute(left, "qbatch", up)
        blocks.append(left)
        if step < ROWS // 2:
            right = lax.ppermute(right, "qbatch", down)
            blocks.append(right)
    passages = fill(passage_lengths, passage_tokens)
    send, back = build(row[None], blocks)
    got = lax.all_to_all(send, "corpus", split_axis=0, concat_axis=0, tiled=True)
    scored = score(me[None], got, passages)
    returned = lax.all_to_all(
        scored.reshape(COLS, VIS, FEAT), "corpus", split_axis=0, concat_axis=0, tiled=True
    )
    mine = hand_back(back, returned.reshape(SLOTS, FEAT))
    parts = lax.all_to_all(
        mine.reshape(ROWS, QDEV, FEAT), "qbatch", split_axis=0, concat_axis=0, tiled=True
    )
    return jnp.sum(parts, axis=0)[:, 0 : VIS * VIS]


def solution(mesh):
    placed = (
        P(("corpus", "qbatch"), None, None),
        P(("corpus", "qbatch"), None),
        P(("corpus", "qbatch"), None, None),
        P(("corpus", "qbatch"), None, None),
        P(("corpus", "qbatch")),
    )
    return jax.shard_map(
        shards, mesh=mesh, in_specs=placed, out_specs=P(("corpus", "qbatch"), None), check_vma=False
    )
```

```python
import jax
import jax.numpy as jnp
from jax import lax
from jax.experimental import pallas as pl
from jax.experimental.pallas import tpu as pltpu
from jax.sharding import PartitionSpec as P

f32, bf16, i32 = jnp.float32, jnp.bfloat16, jnp.int32
TOK = 32
FEAT = 128
PLEN = 128
LOCAL = 64
VIS = 8
HV = VIS // 2
QDEV = 16
ROWS = 8
COLS = 32
GROUP = QDEV * ROWS
SLOTS = COLS * VIS
PIECES = TOK + 1
CELL = VIS * 2 + 1
TILE = 8
TILES = 384
UNROLL = 48
VMEM_LIMIT = 16 * 1024 * 1024


def iota(shape, dim):
    return lax.broadcasted_iota(i32, shape, dim)


def dot_t(a, b, precision=None):
    return lax.dot_general(
        a, b, (((1,), (1,)), ((), ())), precision=precision, preferred_element_type=f32
    )


def dot_n(a, b, precision=None):
    return lax.dot_general(
        a, b, (((1,), (0,)), ((), ())), precision=precision, preferred_element_type=f32
    )


def dot_tn(a, b, precision=None):
    return lax.dot_general(
        a, b, (((0,), (0,)), ((), ())), precision=precision, preferred_element_type=f32
    )


def pack_kernel(tokens_ref, owner_ref, cand_ref, out_ref, owners, cands, sems):
    loads = [
        pltpu.make_async_copy(owner_ref, owners, sems.at[0]),
        pltpu.make_async_copy(cand_ref, cands, sems.at[1]),
        pltpu.make_async_copy(tokens_ref, out_ref.at[pl.ds(0, TOK)], sems.at[2]),
    ]
    for load in loads:
        load.start()
    loads[0].wait()
    loads[1].wait()
    rest = jnp.zeros((FEAT - VIS - VIS * VIS, QDEV), i32)
    lists = jnp.concatenate([owners[...] + 1, cands[...] + 1, rest], 0).astype(bf16)
    eye = (iota((FEAT, FEAT), 0) == iota((FEAT, FEAT), 1)).astype(bf16)
    out_ref[TOK] = dot_tn(lists, eye).astype(bf16)
    loads[2].wait()


def build_kernel(*refs):
    blocks = refs[:ROWS]
    send_ref, back_ref, buf, idx_v, idx_s, idx_sem = refs[ROWS:]
    row = lax.axis_index("qbatch").astype(i32)
    lists = [
        jnp.where(lax.rem(row + step, ROWS) == z, block[TOK].astype(f32), 0.0)
        for z in range(ROWS)
        for block, step in zip(blocks, STEPS)
    ]
    lists = [sum(lists[z * ROWS : z * ROWS + ROWS]) for z in range(ROWS)]
    lists = jnp.concatenate(lists, 0).astype(bf16)
    eye = (iota((GROUP, FEAT), 0) == iota((GROUP, FEAT), 1)).astype(bf16)
    owners = dot_t(eye[0:QDEV], lists)
    wanted = (iota((COLS, GROUP), 0) * ROWS + (row + 1)).astype(f32)
    hit = jnp.zeros((COLS, GROUP), f32)
    for v in range(VIS):
        hit = jnp.where(owners[v : v + 1, :] == wanted, 1.0, hit)
    before = (iota((GROUP, GROUP), 0) < iota((GROUP, GROUP), 1)).astype(bf16)
    rank = dot_n(hit.astype(bf16), before)
    rank = jnp.where(hit > 0.5, rank, -1.0)
    place = iota((COLS, QDEV, GROUP), 1).astype(f32)
    pick = jnp.where(rank[:, None, :] == place, 1.0, 0.0)
    chosen = pick.reshape(COLS * QDEV, GROUP).astype(bf16)
    number = iota((QDEV, GROUP), 1).astype(bf16)
    query = dot_t(number, chosen)[0:8, :].astype(i32)
    idx_v[...] = (query >> 4) * PIECES + (query & (QDEV - 1)) * 2
    to_scalar = pltpu.make_async_copy(idx_v, idx_s, idx_sem)
    to_scalar.start()
    send_ref[:, VIS * 2] = dot_n(chosen, lists).astype(bf16).reshape(COLS, QDEV, FEAT)
    slots = pick[:, 0:VIS, :].reshape(SLOTS, GROUP).astype(bf16)
    back_ref[...] = dot_t(eye, slots)
    for block, step in zip(blocks, STEPS):
        buf[pl.ds(lax.rem(row + step, ROWS) * PIECES, PIECES)] = block[...]
    to_scalar.wait()

    def one(c, _):
        for s in range(VIS):
            send_ref[c, 2 * s : 2 * s + 2] = buf[pl.ds(idx_s[0, c * QDEV + s], 2)]
        return 0

    lax.fori_loop(0, COLS, one, 0)


def split3(x):
    high = x.astype(bf16)
    x = x - high.astype(f32)
    mid = x.astype(bf16)
    return high, mid, (x - mid.astype(f32)).astype(bf16)


def score_kernel(
    got, cells_ref, passage_ref, length_ref, out_ref, held, lengths, plan_v, plan_s, best, sems
):
    load = pltpu.make_async_copy(passage_ref, held, sems.at[0])
    load.start()
    load_lengths = pltpu.make_async_copy(length_ref, lengths, sems.at[2])
    load_lengths.start()
    me = lax.axis_index("corpus") * ROWS + lax.axis_index("qbatch") + 1
    me = me.astype(i32).astype(f32)
    lists = cells_ref[:, VIS * 2].astype(f32)[:, 0:VIS, :].reshape(SLOTS, FEAT)
    lane = iota((SLOTS, FEAT), 1)
    visit = jnp.where((lists == me) & (lane < VIS), 1.0, 0.0).astype(bf16)
    low, high = iota((FEAT, FEAT), 0), iota((FEAT, FEAT), 1)
    spread = ((high >= VIS) & (low == (high >> 3) - 1)).astype(bf16)
    mine = dot_n(visit, spread)
    kept = (lists * mine).astype(bf16)
    k16, l16 = iota((16, FEAT), 0), iota((16, FEAT), 1)
    fold = ((l16 >= VIS) & (l16 < VIS + VIS * VIS) & ((l16 & 7) == k16)).astype(bf16)
    cands = dot_t(fold, kept)

    wide = (LOCAL, SLOTS)
    passage = (iota(wide, 0) + 1).astype(f32)
    slot = iota(wide, 1)
    hit = jnp.zeros(wide, f32)
    for k in range(VIS):
        hit = jnp.where(cands[k : k + 1, :] == passage, 1.0, hit)
    hits = hit.astype(bf16)
    before = (iota((SLOTS, SLOTS), 0) < iota((SLOTS, SLOTS), 1)).astype(bf16)
    rank = dot_n(hits, before).astype(i32)
    count = jnp.sum(hit, axis=1, keepdims=True).astype(i32)
    tiles = (count + (TILE - 1)) >> 3
    tiles_wide = jnp.broadcast_to(tiles, (LOCAL, FEAT)).astype(bf16)
    earlier = (iota((LOCAL, LOCAL), 1) < iota((LOCAL, LOCAL), 0)).astype(bf16)
    first_wide = dot_n(earlier, tiles_wide).astype(i32)
    padded = jnp.concatenate([hits, jnp.zeros(wide, bf16)], 0)
    tiles_row = (dot_t(jnp.ones((16, SLOTS), bf16), padded).astype(i32) + (TILE - 1)) >> 3
    first_row = dot_n(tiles_row.astype(bf16), (low < high).astype(bf16)).astype(i32)
    total = first_row[0:1, FEAT - 1 : FEAT]

    shift = slot - rank
    x = jnp.where(hit > 0.5, shift * 512 + slot + 1, 0)
    for b in range(8):
        moves = ((x >> (9 + b)) & 1) == 1
        x = jnp.where(moves, 0, x) + pltpu.roll(jnp.where(moves, x, 0), SLOTS - (1 << b), 1)
    packed = jnp.maximum((x & 511) - 1, 0).astype(f32).astype(bf16)

    t = iota((TILES, FEAT), 0)
    own = (first_row[0:1] <= t) & (t < first_row[0:1] + tiles_row[0:1])
    own = jnp.where(own, 1.0, 0.0).astype(bf16)
    table = jnp.concatenate(
        [packed, (first_wide >> 4).astype(bf16), (first_wide & 15).astype(bf16)], 1
    )
    rows = dot_n(own[:, 0:LOCAL], table)
    begun = rows[:, SLOTS : SLOTS + FEAT].astype(i32) * 16
    depth = t - begun - rows[:, SLOTS + FEAT :].astype(i32)
    depth = jnp.concatenate([depth, depth], 1)
    here = ((iota((TILES, SLOTS), 1) >> 3) == depth) & (iota((TILES, SLOTS), 0) < total)
    chosen = jnp.where(here, rows[:, 0:SLOTS], 0.0).astype(bf16)
    k16, l16 = iota((16, SLOTS + FEAT), 0), iota((16, SLOTS + FEAT), 1)
    fold = jnp.where((l16 < SLOTS) & ((l16 & 7) == k16), 1.0, 0.0)
    fold = jnp.where((l16 >= SLOTS) & (k16 == TILE), (l16 - SLOTS).astype(f32), fold)
    plan = dot_t(fold.astype(bf16), jnp.concatenate([chosen, own], 1)).astype(i32)
    plan_v[0:TILE, :] = plan[0:TILE] * 2 + (plan[0:TILE] >> 3)
    plan_v[TILE : TILE + 1, :] = plan[TILE : TILE + 1]
    plan_v[TILE + 1 : TILE + 2, :] = jnp.broadcast_to(total, (1, TILES))
    to_scalar = pltpu.make_async_copy(plan_v, plan_s, sems.at[1])
    to_scalar.start()
    to_scalar.wait()
    load_lengths.wait()
    load.wait()
    token = iota((PLEN, FEAT), 0)

    def tile_steps(step, _):
        for half in range(UNROLL // 8):
            found = []
            for u in range(8):
                t = step * UNROLL + half * 8 + u
                queries = jnp.concatenate(
                    [got[pl.ds(plan_s[r, t], 2)].reshape(TOK, FEAT) for r in range(TILE)], 0
                )
                p = plan_s[TILE, t]
                tokens = held[p].astype(f32)
                tokens = jnp.where(token < lengths[p], tokens, tokens[0:1, :]).astype(bf16)
                similarity = dot_t(tokens, queries)
                found.append(jnp.max(similarity, axis=0, keepdims=True))
            at = pl.multiple_of(step * UNROLL + half * 8, 8)
            best[pl.ds(at, 8), :] = jnp.concatenate(found, 0)
        return 0

    lax.fori_loop(0, (plan_s[TILE + 1, 0] + (UNROLL - 1)) // UNROLL, tile_steps, 0)

    adder = ((iota((SLOTS, FEAT), 0) >> 5) == (iota((SLOTS, FEAT), 1) & 7)).astype(bf16)
    sums = dot_n(jnp.concatenate(split3(best[...]), 1), jnp.concatenate([adder] * 3, 0))
    sums = jnp.where(here, jnp.concatenate([sums, sums], 1), 0.0)
    first = first_wide[:, 0:1]
    t = iota((LOCAL, TILES), 1)
    owned = jnp.where((first <= t) & (t < first + tiles), 1.0, 0.0).astype(bf16)
    y = dot_n(jnp.concatenate([owned] * 3, 1), jnp.concatenate(split3(sums), 0))
    y = jnp.where(slot < count, y, 0.0)
    x = x >> 9
    for b in (7, 6, 5, 4, 3, 2, 1, 0):
        moves = ((x >> b) & 1) == 1
        y = jnp.where(moves, 0.0, y) + pltpu.roll(jnp.where(moves, y, 0.0), 1 << b, 1)
        x = jnp.where(moves, 0, x) + pltpu.roll(jnp.where(moves, x, 0), 1 << b, 1)
    scores = jnp.concatenate(
        [
            jnp.sum(jnp.where(cands[k : k + 1, :] == passage, y, 0.0), axis=0, keepdims=True)
            for k in range(VIS)
        ],
        0,
    )
    k8, l8 = iota((VIS, FEAT), 0), iota((VIS, FEAT), 1)
    repeat = ((l8 & 7) == k8).astype(f32)
    spread_back = ((high < VIS * VIS) & (low == (high >> 3))).astype(bf16)
    by_slot = dot_tn(scores, repeat, lax.Precision.HIGHEST)
    by_slot = (by_slot * dot_n(visit, spread_back)).reshape(COLS, VIS, FEAT)
    out_ref[...] = by_slot[:, 0:HV] + pltpu.roll(by_slot[:, HV:VIS], FEAT // 2, 2)


def return_kernel(back_ref, got_ref, out_ref):
    got = got_ref[...]
    lower = iota((COLS, HV, FEAT), 2) < FEAT // 2
    first = jnp.where(lower, got, 0.0)
    second = jnp.where(lower, pltpu.roll(got, FEAT // 2, 2), 0.0)
    by_slot = jnp.concatenate([first, second], 1).reshape(SLOTS, FEAT)
    mine = dot_n(back_ref[...], by_slot, lax.Precision.HIGHEST).reshape(ROWS, QDEV, FEAT)
    out_ref[...] = mine[:, 0:8] + pltpu.roll(mine[:, 8:QDEV], FEAT // 2, 2)


def sum_kernel(parts_ref, out_ref):
    total = jnp.sum(parts_ref[...], axis=0)
    out_ref[0:8] = total[:, 0 : FEAT // 2]
    out_ref[8:QDEV] = total[:, FEAT // 2 : FEAT]


VM = pl.BlockSpec(memory_space=pltpu.VMEM)
ANY = pl.BlockSpec(memory_space=pl.ANY)
PARAMS = pltpu.CompilerParams(vmem_limit_bytes=VMEM_LIMIT)
STEPS = (0, 7, 1, 6, 2, 5, 3, 4)


def in_hbm(x):
    return pltpu.with_memory_space_constraint(x, pltpu.HBM)


def pack(tokens, owners, cands):
    return pl.pallas_call(
        pack_kernel,
        out_shape=jax.ShapeDtypeStruct((PIECES, 16, FEAT), bf16),
        in_specs=[ANY, ANY, ANY],
        out_specs=VM,
        scratch_shapes=[
            pltpu.VMEM((VIS, QDEV), i32),
            pltpu.VMEM((VIS * VIS, QDEV), i32),
            pltpu.SemaphoreType.DMA((3,)),
        ],
        compiler_params=PARAMS,
    )(in_hbm(tokens), in_hbm(owners), in_hbm(cands))


def build(blocks):
    return pl.pallas_call(
        build_kernel,
        out_shape=(
            jax.ShapeDtypeStruct((COLS, CELL, 16, FEAT), bf16),
            jax.ShapeDtypeStruct((GROUP, SLOTS), f32),
        ),
        in_specs=[VM] * ROWS,
        out_specs=(VM, VM),
        scratch_shapes=[
            pltpu.VMEM((ROWS * PIECES, 16, FEAT), bf16),
            pltpu.VMEM((8, COLS * QDEV), i32),
            pltpu.SMEM((8, COLS * QDEV), i32),
            pltpu.SemaphoreType.DMA,
        ],
        compiler_params=PARAMS,
    )(*blocks)


def score(got, passages, lengths):
    return pl.pallas_call(
        score_kernel,
        out_shape=jax.ShapeDtypeStruct((COLS, HV, FEAT), f32),
        in_specs=[VM, VM, ANY, ANY],
        out_specs=VM,
        scratch_shapes=[
            pltpu.VMEM((LOCAL, PLEN, FEAT), bf16),
            pltpu.SMEM((LOCAL,), i32),
            pltpu.VMEM((16, TILES), i32),
            pltpu.SMEM((16, TILES), i32),
            pltpu.VMEM((TILES, SLOTS), f32),
            pltpu.SemaphoreType.DMA((3,)),
        ],
        compiler_params=PARAMS,
    )(got.reshape(COLS * CELL, 16, FEAT), got, in_hbm(passages), in_hbm(lengths))


def hand_back(back, got):
    return pl.pallas_call(
        return_kernel,
        out_shape=jax.ShapeDtypeStruct((ROWS, 8, FEAT), f32),
        in_specs=[VM, VM],
        out_specs=VM,
        compiler_params=PARAMS,
    )(back, got)


def add_up(parts):
    return pl.pallas_call(
        sum_kernel,
        out_shape=jax.ShapeDtypeStruct((QDEV, VIS * VIS), f32),
        in_specs=[VM],
        out_specs=VM,
        compiler_params=PARAMS,
    )(parts)


def shards(query_tokens, visit_owner, visit_passages, passage_tokens, passage_lengths):
    own = pack(
        query_tokens.reshape(TOK, 16, FEAT),
        visit_owner.T,
        jnp.transpose(visit_passages, (1, 2, 0)).reshape(VIS * VIS, QDEV),
    )
    up = [(i, (i + 1) % ROWS) for i in range(ROWS)]
    down = [(i, (i + ROWS - 1) % ROWS) for i in range(ROWS)]
    blocks = [own]
    left = right = own
    for step in range(1, ROWS // 2 + 1):
        left = lax.ppermute(left, "qbatch", up)
        blocks.append(left)
        if step < ROWS // 2:
            right = lax.ppermute(right, "qbatch", down)
            blocks.append(right)
    send, back = build(blocks)
    got = lax.all_to_all(send, "corpus", split_axis=0, concat_axis=0, tiled=True)
    scored = score(got, passage_tokens, passage_lengths)
    returned = lax.all_to_all(scored, "corpus", split_axis=0, concat_axis=0, tiled=True)
    mine = hand_back(back, returned)
    return add_up(lax.all_to_all(mine, "qbatch", split_axis=0, concat_axis=0, tiled=True))


def solution(mesh):
    placed = (
        P(("corpus", "qbatch"), None, None),
        P(("corpus", "qbatch"), None),
        P(("corpus", "qbatch"), None, None),
        P(("corpus", "qbatch"), None, None),
        P(("corpus", "qbatch")),
    )
    return jax.shard_map(
        shards, mesh=mesh, in_specs=placed, out_specs=P(("corpus", "qbatch"), None), check_vma=False
    )
```

```python
import jax
import jax.numpy as jnp
from jax import lax
from jax.experimental import pallas as pl
from jax.experimental.pallas import tpu as pltpu
from jax.sharding import PartitionSpec as P

f32, bf16, i32 = jnp.float32, jnp.bfloat16, jnp.int32
TOK = 32
FEAT = 128
PLEN = 128
LOCAL = 64
VIS = 8
HV = VIS // 2
QDEV = 16
ROWS = 8
COLS = 32
GROUP = QDEV * ROWS
SLOTS = COLS * VIS
PIECES = TOK + 1
CELL = VIS * 2 + 1
TILE = 8
TILES = 384
UNROLL = 72
VMEM_LIMIT = 16 * 1024 * 1024


def iota(shape, dim):
    return lax.broadcasted_iota(i32, shape, dim)


def dot_t(a, b, precision=None):
    return lax.dot_general(
        a, b, (((1,), (1,)), ((), ())), precision=precision, preferred_element_type=f32
    )


def dot_n(a, b, precision=None):
    return lax.dot_general(
        a, b, (((1,), (0,)), ((), ())), precision=precision, preferred_element_type=f32
    )


def dot_tn(a, b, precision=None):
    return lax.dot_general(
        a, b, (((0,), (0,)), ((), ())), precision=precision, preferred_element_type=f32
    )


def pack_kernel(tokens_ref, owner_ref, cand_ref, out_ref, owners, cands, sems):
    loads = [
        pltpu.make_async_copy(owner_ref, owners, sems.at[0]),
        pltpu.make_async_copy(cand_ref, cands, sems.at[1]),
        pltpu.make_async_copy(tokens_ref, out_ref.at[pl.ds(0, TOK)], sems.at[2]),
    ]
    for load in loads:
        load.start()
    loads[0].wait()
    loads[1].wait()
    rest = jnp.zeros((FEAT - VIS - VIS * VIS, QDEV), i32)
    lists = jnp.concatenate([owners[...] + 1, cands[...] + 1, rest], 0).astype(bf16)
    eye = (iota((FEAT, FEAT), 0) == iota((FEAT, FEAT), 1)).astype(bf16)
    out_ref[TOK] = dot_tn(lists, eye).astype(bf16)
    loads[2].wait()


def build_kernel(*refs):
    blocks = refs[:ROWS]
    send_ref, back_ref, buf, idx_v, idx_s, idx_sem = refs[ROWS:]
    row = lax.axis_index("qbatch").astype(i32)
    lists = [
        jnp.where(lax.rem(row + step, ROWS) == z, block[TOK].astype(f32), 0.0)
        for z in range(ROWS)
        for block, step in zip(blocks, STEPS)
    ]
    lists = [sum(lists[z * ROWS : z * ROWS + ROWS]) for z in range(ROWS)]
    lists = jnp.concatenate(lists, 0).astype(bf16)
    eye = (iota((GROUP, FEAT), 0) == iota((GROUP, FEAT), 1)).astype(bf16)
    owners = dot_t(eye[0:QDEV], lists)
    wanted = (iota((COLS, GROUP), 0) * ROWS + (row + 1)).astype(f32)
    hit = jnp.zeros((COLS, GROUP), f32)
    for v in range(VIS):
        hit = jnp.where(owners[v : v + 1, :] == wanted, 1.0, hit)
    before = (iota((GROUP, GROUP), 0) < iota((GROUP, GROUP), 1)).astype(bf16)
    rank = dot_n(hit.astype(bf16), before)
    rank = jnp.where(hit > 0.5, rank, -1.0)
    place = iota((COLS, QDEV, GROUP), 1).astype(f32)
    pick = jnp.where(rank[:, None, :] == place, 1.0, 0.0)
    chosen = pick.reshape(COLS * QDEV, GROUP).astype(bf16)
    number = iota((QDEV, GROUP), 1).astype(bf16)
    query = dot_t(number, chosen)[0:8, :].astype(i32)
    idx_v[...] = (query >> 4) * PIECES + (query & (QDEV - 1)) * 2
    to_scalar = pltpu.make_async_copy(idx_v, idx_s, idx_sem)
    to_scalar.start()
    rows = dot_n(chosen, lists)
    lane = iota((COLS * QDEV, FEAT), 1)
    target = ((iota((COLS * QDEV, FEAT), 0) >> 4) * ROWS + (row + 1)).astype(f32)
    visit = jnp.where((rows == target) & (lane < VIS), 1.0, 0.0).astype(bf16)
    low, high = iota((FEAT, FEAT), 0), iota((FEAT, FEAT), 1)
    spread = ((high >= VIS) & (low == (high >> 3) - 1)).astype(bf16)
    kept = (rows * dot_n(visit, spread)).astype(bf16)
    send_ref[:, VIS * 2] = kept.reshape(COLS, QDEV, FEAT)
    slots = pick[:, 0:VIS, :].reshape(SLOTS, GROUP).astype(bf16)
    back_ref[...] = dot_t(eye, slots)
    for block, step in zip(blocks, STEPS):
        buf[pl.ds(lax.rem(row + step, ROWS) * PIECES, PIECES)] = block[...]
    to_scalar.wait()

    def one(c, _):
        for s in range(VIS):
            send_ref[c, 2 * s : 2 * s + 2] = buf[pl.ds(idx_s[0, c * QDEV + s], 2)]
        return 0

    lax.fori_loop(0, COLS, one, 0)


def split3(x):
    high = x.astype(bf16)
    x = x - high.astype(f32)
    mid = x.astype(bf16)
    return high, mid, (x - mid.astype(f32)).astype(bf16)


def score_kernel(
    got, cells_ref, passage_ref, length_ref, out_ref, held, lengths, plan_v, plan_s, best, sems
):
    load = pltpu.make_async_copy(passage_ref, held, sems.at[0])
    load.start()
    load_lengths = pltpu.make_async_copy(length_ref, lengths, sems.at[2])
    load_lengths.start()
    kept = cells_ref[:, VIS * 2].astype(f32)[:, 0:VIS, :].reshape(SLOTS, FEAT)
    low, high = iota((FEAT, FEAT), 0), iota((FEAT, FEAT), 1)
    k16, l16 = iota((16, FEAT), 0), iota((16, FEAT), 1)
    fold = ((l16 >= VIS) & (l16 < VIS + VIS * VIS) & ((l16 & 7) == k16)).astype(bf16)
    cands = dot_t(fold, kept.astype(bf16))

    wide = (LOCAL, SLOTS)
    passage = (iota(wide, 0) + 1).astype(f32)
    slot = iota(wide, 1)
    hit = jnp.zeros(wide, f32)
    for k in range(VIS):
        hit = jnp.where(cands[k : k + 1, :] == passage, 1.0, hit)
    hits = hit.astype(bf16)
    before = (iota((SLOTS, SLOTS), 0) < iota((SLOTS, SLOTS), 1)).astype(bf16)
    rank = dot_n(hits, before).astype(i32)
    count = jnp.sum(hit, axis=1, keepdims=True).astype(i32)
    tiles = (count + (TILE - 1)) >> 3
    tiles_wide = jnp.broadcast_to(tiles, (LOCAL, FEAT)).astype(bf16)
    earlier = (iota((LOCAL, LOCAL), 1) < iota((LOCAL, LOCAL), 0)).astype(bf16)
    first_wide = dot_n(earlier, tiles_wide).astype(i32)
    padded = jnp.concatenate([hits, jnp.zeros(wide, bf16)], 0)
    tiles_row = (dot_t(jnp.ones((16, SLOTS), bf16), padded).astype(i32) + (TILE - 1)) >> 3
    first_row = dot_n(tiles_row.astype(bf16), (low < high).astype(bf16)).astype(i32)
    total = first_row[0:1, FEAT - 1 : FEAT]

    shift = slot - rank
    x = jnp.where(hit > 0.5, shift * 512 + slot + 1, 0)
    for b in range(8):
        moves = ((x >> (9 + b)) & 1) == 1
        x = jnp.where(moves, 0, x) + pltpu.roll(jnp.where(moves, x, 0), SLOTS - (1 << b), 1)
    packed = jnp.maximum((x & 511) - 1, 0).astype(f32).astype(bf16)

    t = iota((TILES, FEAT), 0)
    own = (first_row[0:1] <= t) & (t < first_row[0:1] + tiles_row[0:1])
    own = jnp.where(own, 1.0, 0.0).astype(bf16)
    table = jnp.concatenate(
        [packed, (first_wide >> 4).astype(bf16), (first_wide & 15).astype(bf16)], 1
    )
    rows = dot_n(own[:, 0:LOCAL], table)
    begun = rows[:, SLOTS : SLOTS + FEAT].astype(i32) * 16
    depth = t - begun - rows[:, SLOTS + FEAT :].astype(i32)
    depth = jnp.concatenate([depth, depth], 1)
    here = ((iota((TILES, SLOTS), 1) >> 3) == depth) & (iota((TILES, SLOTS), 0) < total)
    chosen = jnp.where(here, rows[:, 0:SLOTS], 0.0).astype(bf16)
    k16, l16 = iota((16, SLOTS + FEAT), 0), iota((16, SLOTS + FEAT), 1)
    fold = jnp.where((l16 < SLOTS) & ((l16 & 7) == k16), 1.0, 0.0)
    fold = jnp.where((l16 >= SLOTS) & (k16 == TILE), (l16 - SLOTS).astype(f32), fold)
    plan = dot_t(fold.astype(bf16), jnp.concatenate([chosen, own], 1)).astype(i32)
    plan_v[0:TILE, :] = plan[0:TILE] * 2 + (plan[0:TILE] >> 3)
    plan_v[TILE : TILE + 1, :] = plan[TILE : TILE + 1]
    plan_v[TILE + 1 : TILE + 2, :] = jnp.broadcast_to(total, (1, TILES))
    to_scalar = pltpu.make_async_copy(plan_v, plan_s, sems.at[1])
    to_scalar.start()
    adder = ((iota((SLOTS, FEAT), 0) >> 5) == (iota((SLOTS, FEAT), 1) & 7)).astype(bf16)
    first = first_wide[:, 0:1]
    t = iota((LOCAL, TILES), 1)
    owned = jnp.where((first <= t) & (t < first + tiles), 1.0, 0.0).astype(bf16)
    to_scalar.wait()
    load_lengths.wait()
    load.wait()
    token = iota((PLEN, FEAT), 0)

    def tile_steps(step, _):
        for half in range(UNROLL // 8):
            found = []
            for u in range(8):
                t = step * UNROLL + half * 8 + u
                queries = jnp.concatenate(
                    [got[pl.ds(plan_s[r, t], 2)].reshape(TOK, FEAT) for r in range(TILE)], 0
                )
                p = plan_s[TILE, t]
                tokens = held[p].astype(f32)
                tokens = jnp.where(token < lengths[p], tokens, tokens[0:1, :]).astype(bf16)
                similarity = dot_t(tokens, queries)
                found.append(jnp.max(similarity, axis=0, keepdims=True))
            at = pl.multiple_of(step * UNROLL + half * 8, 8)
            best[pl.ds(at, 8), :] = jnp.concatenate(found, 0)
        return 0

    lax.fori_loop(0, (plan_s[TILE + 1, 0] + (UNROLL - 1)) // UNROLL, tile_steps, 0)

    sums = dot_n(jnp.concatenate(split3(best[...]), 1), jnp.concatenate([adder] * 3, 0))
    sums = jnp.where(here, jnp.concatenate([sums, sums], 1), 0.0)
    y = dot_n(jnp.concatenate([owned] * 3, 1), jnp.concatenate(split3(sums), 0))
    y = jnp.where(slot < count, y, 0.0)
    x = x >> 9
    for b in (7, 6, 5, 4, 3, 2, 1, 0):
        moves = ((x >> b) & 1) == 1
        y = jnp.where(moves, 0.0, y) + pltpu.roll(jnp.where(moves, y, 0.0), 1 << b, 1)
        x = jnp.where(moves, 0, x) + pltpu.roll(jnp.where(moves, x, 0), 1 << b, 1)
    scores = jnp.concatenate(
        [
            jnp.sum(jnp.where(cands[k : k + 1, :] == passage, y, 0.0), axis=0, keepdims=True)
            for k in range(VIS)
        ],
        0,
    )
    k8, l8 = iota((VIS, FEAT), 0), iota((VIS, FEAT), 1)
    repeat = ((l8 & 7) == k8).astype(f32)
    by_slot = dot_tn(scores, repeat, lax.Precision.HIGHEST)
    mine = pltpu.roll(kept, FEAT - VIS, 1) > 0.5
    by_slot = jnp.where(mine, by_slot, 0.0).reshape(COLS, VIS, FEAT)
    out_ref[...] = by_slot[:, 0:HV] + pltpu.roll(by_slot[:, HV:VIS], FEAT // 2, 2)


def return_kernel(back_ref, got_ref, out_ref):
    got = got_ref[...]
    lower = iota((COLS, HV, FEAT), 2) < FEAT // 2
    first = jnp.where(lower, got, 0.0)
    second = jnp.where(lower, pltpu.roll(got, FEAT // 2, 2), 0.0)
    by_slot = jnp.concatenate([first, second], 1).reshape(SLOTS, FEAT)
    mine = dot_n(back_ref[...], by_slot, lax.Precision.HIGHEST).reshape(ROWS, QDEV, FEAT)
    out_ref[...] = mine[:, 0:8] + pltpu.roll(mine[:, 8:QDEV], FEAT // 2, 2)


def sum_kernel(parts_ref, out_ref):
    total = jnp.sum(parts_ref[...], axis=0)
    out_ref[0:8] = total[:, 0 : FEAT // 2]
    out_ref[8:QDEV] = total[:, FEAT // 2 : FEAT]


VM = pl.BlockSpec(memory_space=pltpu.VMEM)
ANY = pl.BlockSpec(memory_space=pl.ANY)
PARAMS = pltpu.CompilerParams(vmem_limit_bytes=VMEM_LIMIT)
STEPS = (0, 7, 1, 6, 2, 5, 3, 4)


def in_hbm(x):
    return pltpu.with_memory_space_constraint(x, pltpu.HBM)


def pack(tokens, owners, cands):
    return pl.pallas_call(
        pack_kernel,
        out_shape=jax.ShapeDtypeStruct((PIECES, 16, FEAT), bf16),
        in_specs=[ANY, ANY, ANY],
        out_specs=VM,
        scratch_shapes=[
            pltpu.VMEM((VIS, QDEV), i32),
            pltpu.VMEM((VIS * VIS, QDEV), i32),
            pltpu.SemaphoreType.DMA((3,)),
        ],
        compiler_params=PARAMS,
    )(in_hbm(tokens), in_hbm(owners), in_hbm(cands))


def build(blocks):
    return pl.pallas_call(
        build_kernel,
        out_shape=(
            jax.ShapeDtypeStruct((COLS, CELL, 16, FEAT), bf16),
            jax.ShapeDtypeStruct((GROUP, SLOTS), f32),
        ),
        in_specs=[VM] * ROWS,
        out_specs=(VM, VM),
        scratch_shapes=[
            pltpu.VMEM((ROWS * PIECES, 16, FEAT), bf16),
            pltpu.VMEM((8, COLS * QDEV), i32),
            pltpu.SMEM((8, COLS * QDEV), i32),
            pltpu.SemaphoreType.DMA,
        ],
        compiler_params=PARAMS,
    )(*blocks)


def score(got, passages, lengths):
    return pl.pallas_call(
        score_kernel,
        out_shape=jax.ShapeDtypeStruct((COLS, HV, FEAT), f32),
        in_specs=[VM, VM, ANY, ANY],
        out_specs=VM,
        scratch_shapes=[
            pltpu.VMEM((LOCAL, PLEN, FEAT), bf16),
            pltpu.SMEM((LOCAL,), i32),
            pltpu.VMEM((16, TILES), i32),
            pltpu.SMEM((16, TILES), i32),
            pltpu.VMEM((TILES, SLOTS), f32),
            pltpu.SemaphoreType.DMA((3,)),
        ],
        compiler_params=PARAMS,
    )(got.reshape(COLS * CELL, 16, FEAT), got, in_hbm(passages), in_hbm(lengths))


def hand_back(back, got):
    return pl.pallas_call(
        return_kernel,
        out_shape=jax.ShapeDtypeStruct((ROWS, 8, FEAT), f32),
        in_specs=[VM, VM],
        out_specs=VM,
        compiler_params=PARAMS,
    )(back, got)


def add_up(parts):
    return pl.pallas_call(
        sum_kernel,
        out_shape=jax.ShapeDtypeStruct((QDEV, VIS * VIS), f32),
        in_specs=[VM],
        out_specs=VM,
        compiler_params=PARAMS,
    )(parts)


def shards(query_tokens, visit_owner, visit_passages, passage_tokens, passage_lengths):
    own = pack(
        query_tokens.reshape(TOK, 16, FEAT),
        visit_owner.T,
        jnp.transpose(visit_passages, (1, 2, 0)).reshape(VIS * VIS, QDEV),
    )
    up = [(i, (i + 1) % ROWS) for i in range(ROWS)]
    down = [(i, (i + ROWS - 1) % ROWS) for i in range(ROWS)]
    blocks = [own]
    left = right = own
    for step in range(1, ROWS // 2):
        left = lax.ppermute(left, "qbatch", up)
        right = lax.ppermute(right, "qbatch", down)
        if step == 1:
            right, again = lax.optimization_barrier((right, own))
            far = lax.ppermute(again, "qbatch", [(i, (i + ROWS // 2) % ROWS) for i in range(ROWS)])
        blocks += [left, right]
    blocks.append(far)
    send, back = build(blocks)
    got = lax.all_to_all(send, "corpus", split_axis=0, concat_axis=0, tiled=True)
    scored = score(got, passage_tokens, passage_lengths)
    returned = lax.all_to_all(scored, "corpus", split_axis=0, concat_axis=0, tiled=True)
    mine = hand_back(back, returned)
    return add_up(lax.all_to_all(mine, "qbatch", split_axis=0, concat_axis=0, tiled=True))


def solution(mesh):
    placed = (
        P(("corpus", "qbatch"), None, None),
        P(("corpus", "qbatch"), None),
        P(("corpus", "qbatch"), None, None),
        P(("corpus", "qbatch"), None, None),
        P(("corpus", "qbatch")),
    )
    return jax.shard_map(
        shards, mesh=mesh, in_specs=placed, out_specs=P(("corpus", "qbatch"), None), check_vma=False
    )
```

```python
import jax
import jax.numpy as jnp
from jax import lax
from jax.experimental import pallas as pl
from jax.experimental.pallas import tpu as pltpu
from jax.sharding import PartitionSpec as P

f32, bf16, i32 = jnp.float32, jnp.bfloat16, jnp.int32
TOK = 32
FEAT = 128
PLEN = 128
LOCAL = 64
VIS = 8
QDEV = 16
ROWS = 8
COLS = 32
GROUP = QDEV * ROWS
OWNERS = COLS * ROWS
SLOTS = COLS * VIS
PIECES = TOK + 1
CELL = VIS * 2 + 1
TILE = 8
TILES = 384
UNROLL = 72
VMEM_LIMIT = 16 * 1024 * 1024


def iota(shape, dim):
    return lax.broadcasted_iota(i32, shape, dim)


def dot_t(a, b, precision=None):
    return lax.dot_general(
        a, b, (((1,), (1,)), ((), ())), precision=precision, preferred_element_type=f32
    )


def dot_n(a, b, precision=None):
    return lax.dot_general(
        a, b, (((1,), (0,)), ((), ())), precision=precision, preferred_element_type=f32
    )


def dot_tn(a, b, precision=None):
    return lax.dot_general(
        a, b, (((0,), (0,)), ((), ())), precision=precision, preferred_element_type=f32
    )


def pack_kernel(tokens_ref, owner_ref, cand_ref, out_ref, owners, cands, sems):
    loads = [
        pltpu.make_async_copy(owner_ref, owners, sems.at[0]),
        pltpu.make_async_copy(cand_ref, cands, sems.at[1]),
        pltpu.make_async_copy(tokens_ref, out_ref.at[pl.ds(0, TOK)], sems.at[2]),
    ]
    for load in loads:
        load.start()
    loads[0].wait()
    loads[1].wait()
    rest = jnp.zeros((FEAT - VIS - VIS * VIS, QDEV), i32)
    lists = jnp.concatenate([owners[...] + 1, cands[...] + 1, rest], 0).astype(bf16)
    eye = (iota((FEAT, FEAT), 0) == iota((FEAT, FEAT), 1)).astype(bf16)
    out_ref[TOK] = dot_tn(lists, eye).astype(bf16)
    loads[2].wait()


def build_kernel(*refs):
    blocks = refs[:ROWS]
    send_ref, pick_ref, mask_ref, buf, idx_v, idx_s, idx_sem = refs[ROWS:]
    row = lax.axis_index("qbatch").astype(i32)
    lists = [
        jnp.where(lax.rem(row + step, ROWS) == z, block[TOK].astype(f32), 0.0)
        for z in range(ROWS)
        for block, step in zip(blocks, STEPS)
    ]
    lists = [sum(lists[z * ROWS : z * ROWS + ROWS]) for z in range(ROWS)]
    lists = jnp.concatenate(lists, 0).astype(bf16)
    eye = (iota((GROUP, FEAT), 0) == iota((GROUP, FEAT), 1)).astype(bf16)
    owners = dot_t(eye[0:QDEV], lists)
    wanted = (iota((COLS, GROUP), 0) * ROWS + (row + 1)).astype(f32)
    hit = jnp.zeros((COLS, GROUP), f32)
    for v in range(VIS):
        hit = jnp.where(owners[v : v + 1, :] == wanted, 1.0, hit)
    before = (iota((GROUP, GROUP), 0) < iota((GROUP, GROUP), 1)).astype(bf16)
    rank = dot_n(hit.astype(bf16), before)
    rank = jnp.where(hit > 0.5, rank, -1.0)
    place = iota((COLS, QDEV, GROUP), 1).astype(f32)
    pick = jnp.where(rank[:, None, :] == place, 1.0, 0.0)
    chosen = pick.reshape(COLS * QDEV, GROUP).astype(bf16)
    number = iota((QDEV, GROUP), 1).astype(bf16)
    query = dot_t(number, chosen)[0:8, :].astype(i32)
    idx_v[...] = (query >> 4) * PIECES + (query & (QDEV - 1)) * 2
    to_scalar = pltpu.make_async_copy(idx_v, idx_s, idx_sem)
    to_scalar.start()
    rows = dot_n(chosen, lists)
    lane = iota((COLS * QDEV, FEAT), 1)
    target = ((iota((COLS * QDEV, FEAT), 0) >> 4) * ROWS + (row + 1)).astype(f32)
    visit = jnp.where((rows == target) & (lane < VIS), 1.0, 0.0).astype(bf16)
    low, high = iota((FEAT, FEAT), 0), iota((FEAT, FEAT), 1)
    spread = ((high >= VIS) & (low == (high >> 3) - 1)).astype(bf16)
    kept = (rows * dot_n(visit, spread)).astype(bf16)
    send_ref[:, VIS * 2] = kept.reshape(COLS, QDEV, FEAT)
    every = (iota((GROUP, OWNERS), 1) + 1).astype(f32)
    theirs = lists.astype(f32)
    visited = jnp.zeros((GROUP, OWNERS), f32)
    for v in range(VIS):
        visited = jnp.where(theirs[:, v : v + 1] == every, 1.0, visited)
    earlier = (iota((QDEV, GROUP), 1) < iota((QDEV, GROUP), 0) + row * QDEV).astype(bf16)
    places = dot_n(earlier, visited.astype(bf16))
    ours = blocks[0][TOK].astype(f32)
    lane = iota((QDEV, FEAT), 1)
    for v in range(VIS):
        at = jnp.where(ours[:, v : v + 1] == every[0:QDEV], 1.0, 0.0)
        pick_ref[v * QDEV : (v + 1) * QDEV, :] = at.astype(bf16)
        place = jnp.sum(at * places, axis=1, keepdims=True).astype(i32)
        mask_ref[v * QDEV : (v + 1) * QDEV, :] = jnp.where((lane >> 3) == place, 1.0, 0.0)
    for block, step in zip(blocks, STEPS):
        buf[pl.ds(lax.rem(row + step, ROWS) * PIECES, PIECES)] = block[...]
    to_scalar.wait()

    def one(c, _):
        for s in range(VIS):
            send_ref[c, 2 * s : 2 * s + 2] = buf[pl.ds(idx_s[0, c * QDEV + s], 2)]
        return 0

    lax.fori_loop(0, COLS, one, 0)


def split3(x):
    high = x.astype(bf16)
    x = x - high.astype(f32)
    mid = x.astype(bf16)
    return high, mid, (x - mid.astype(f32)).astype(bf16)


def score_kernel(
    got, cells_ref, passage_ref, length_ref, out_ref, held, lengths, plan_v, plan_s, best, sems
):
    load = pltpu.make_async_copy(passage_ref, held, sems.at[0])
    load.start()
    load_lengths = pltpu.make_async_copy(length_ref, lengths, sems.at[2])
    load_lengths.start()
    kept = cells_ref[:, VIS * 2].astype(f32)[:, 0:VIS, :].reshape(SLOTS, FEAT)
    low, high = iota((FEAT, FEAT), 0), iota((FEAT, FEAT), 1)
    k16, l16 = iota((16, FEAT), 0), iota((16, FEAT), 1)
    fold = ((l16 >= VIS) & (l16 < VIS + VIS * VIS) & ((l16 & 7) == k16)).astype(bf16)
    cands = dot_t(fold, kept.astype(bf16))

    wide = (LOCAL, SLOTS)
    passage = (iota(wide, 0) + 1).astype(f32)
    slot = iota(wide, 1)
    hit = jnp.zeros(wide, f32)
    for k in range(VIS):
        hit = jnp.where(cands[k : k + 1, :] == passage, 1.0, hit)
    hits = hit.astype(bf16)
    before = (iota((SLOTS, SLOTS), 0) < iota((SLOTS, SLOTS), 1)).astype(bf16)
    rank = dot_n(hits, before).astype(i32)
    count = jnp.sum(hit, axis=1, keepdims=True).astype(i32)
    tiles = (count + (TILE - 1)) >> 3
    tiles_wide = jnp.broadcast_to(tiles, (LOCAL, FEAT)).astype(bf16)
    earlier = (iota((LOCAL, LOCAL), 1) < iota((LOCAL, LOCAL), 0)).astype(bf16)
    first_wide = dot_n(earlier, tiles_wide).astype(i32)
    padded = jnp.concatenate([hits, jnp.zeros(wide, bf16)], 0)
    tiles_row = (dot_t(jnp.ones((16, SLOTS), bf16), padded).astype(i32) + (TILE - 1)) >> 3
    first_row = dot_n(tiles_row.astype(bf16), (low < high).astype(bf16)).astype(i32)
    total = first_row[0:1, FEAT - 1 : FEAT]

    shift = slot - rank
    x = jnp.where(hit > 0.5, shift * 512 + slot + 1, 0)
    for b in range(8):
        moves = ((x >> (9 + b)) & 1) == 1
        x = jnp.where(moves, 0, x) + pltpu.roll(jnp.where(moves, x, 0), SLOTS - (1 << b), 1)
    packed = jnp.maximum((x & 511) - 1, 0).astype(f32).astype(bf16)

    t = iota((TILES, FEAT), 0)
    own = (first_row[0:1] <= t) & (t < first_row[0:1] + tiles_row[0:1])
    own = jnp.where(own, 1.0, 0.0).astype(bf16)
    table = jnp.concatenate(
        [packed, (first_wide >> 4).astype(bf16), (first_wide & 15).astype(bf16)], 1
    )
    rows = dot_n(own[:, 0:LOCAL], table)
    begun = rows[:, SLOTS : SLOTS + FEAT].astype(i32) * 16
    depth = t - begun - rows[:, SLOTS + FEAT :].astype(i32)
    depth = jnp.concatenate([depth, depth], 1)
    here = ((iota((TILES, SLOTS), 1) >> 3) == depth) & (iota((TILES, SLOTS), 0) < total)
    chosen = jnp.where(here, rows[:, 0:SLOTS], 0.0).astype(bf16)
    k16, l16 = iota((16, SLOTS + FEAT), 0), iota((16, SLOTS + FEAT), 1)
    fold = jnp.where((l16 < SLOTS) & ((l16 & 7) == k16), 1.0, 0.0)
    fold = jnp.where((l16 >= SLOTS) & (k16 == TILE), (l16 - SLOTS).astype(f32), fold)
    plan = dot_t(fold.astype(bf16), jnp.concatenate([chosen, own], 1)).astype(i32)
    plan_v[0:TILE, :] = plan[0:TILE] * 2 + (plan[0:TILE] >> 3)
    plan_v[TILE : TILE + 1, :] = plan[TILE : TILE + 1]
    plan_v[TILE + 1 : TILE + 2, :] = jnp.broadcast_to(total, (1, TILES))
    to_scalar = pltpu.make_async_copy(plan_v, plan_s, sems.at[1])
    to_scalar.start()
    adder = ((iota((SLOTS, FEAT), 0) >> 5) == (iota((SLOTS, FEAT), 1) & 7)).astype(bf16)
    first = first_wide[:, 0:1]
    t = iota((LOCAL, TILES), 1)
    owned = jnp.where((first <= t) & (t < first + tiles), 1.0, 0.0).astype(bf16)
    to_scalar.wait()
    load_lengths.wait()
    load.wait()
    token = iota((PLEN, FEAT), 0)

    def tile_steps(step, _):
        for half in range(UNROLL // 8):
            found = []
            for u in range(8):
                t = step * UNROLL + half * 8 + u
                queries = jnp.concatenate(
                    [got[pl.ds(plan_s[r, t], 2)].reshape(TOK, FEAT) for r in range(TILE)], 0
                )
                p = plan_s[TILE, t]
                tokens = held[p].astype(f32)
                tokens = jnp.where(token < lengths[p], tokens, tokens[0:1, :]).astype(bf16)
                similarity = dot_t(tokens, queries)
                found.append(jnp.max(similarity, axis=0, keepdims=True))
            at = pl.multiple_of(step * UNROLL + half * 8, 8)
            best[pl.ds(at, 8), :] = jnp.concatenate(found, 0)
        return 0

    lax.fori_loop(0, (plan_s[TILE + 1, 0] + (UNROLL - 1)) // UNROLL, tile_steps, 0)

    sums = dot_n(jnp.concatenate(split3(best[...]), 1), jnp.concatenate([adder] * 3, 0))
    sums = jnp.where(here, jnp.concatenate([sums, sums], 1), 0.0)
    y = dot_n(jnp.concatenate([owned] * 3, 1), jnp.concatenate(split3(sums), 0))
    y = jnp.where(slot < count, y, 0.0)
    x = x >> 9
    for b in (7, 6, 5, 4, 3, 2, 1, 0):
        moves = ((x >> b) & 1) == 1
        y = jnp.where(moves, 0.0, y) + pltpu.roll(jnp.where(moves, y, 0.0), 1 << b, 1)
        x = jnp.where(moves, 0, x) + pltpu.roll(jnp.where(moves, x, 0), 1 << b, 1)
    scores = jnp.concatenate(
        [
            jnp.sum(jnp.where(cands[k : k + 1, :] == passage, y, 0.0), axis=0, keepdims=True)
            for k in range(VIS)
        ],
        0,
    )
    k8, l8 = iota((VIS, FEAT), 0), iota((VIS, FEAT), 1)
    repeat = ((l8 & 7) == k8).astype(f32)
    by_slot = dot_tn(scores, repeat, lax.Precision.HIGHEST)
    lane = iota((SLOTS, FEAT), 1)
    by_slot = jnp.where((lane >> 3) == (iota((SLOTS, FEAT), 0) & 7), by_slot, 0.0)
    by_group = jnp.sum(by_slot.reshape(COLS, VIS, FEAT), axis=1, keepdims=True)
    out_ref[...] = jnp.broadcast_to(by_group[:, None], (COLS, ROWS, 1, FEAT))


def return_kernel(pick_ref, mask_ref, got_ref, out_ref):
    pick = pick_ref[...]
    found = dot_n(jnp.concatenate([pick] * 3, 1), jnp.concatenate(split3(got_ref[...]), 0))
    found = jnp.where(mask_ref[...] > 0.5, found, 0.0)
    for step in (8, 16, 32, 64):
        found = found + pltpu.roll(found, step, 1)
    shape = (QDEV * VIS, FEAT)
    found = jnp.where((iota(shape, 1) >> 3) == (iota(shape, 0) >> 4), found, 0.0)
    out_ref[...] = jnp.sum(found.reshape(VIS, QDEV, FEAT), axis=0)[:, 0 : VIS * VIS]


VM = pl.BlockSpec(memory_space=pltpu.VMEM)
ANY = pl.BlockSpec(memory_space=pl.ANY)
PARAMS = pltpu.CompilerParams(vmem_limit_bytes=VMEM_LIMIT)
STEPS = (0, 7, 1, 6, 2, 5, 3, 4)


def in_hbm(x):
    return pltpu.with_memory_space_constraint(x, pltpu.HBM)


def pack(tokens, owners, cands):
    return pl.pallas_call(
        pack_kernel,
        out_shape=jax.ShapeDtypeStruct((PIECES, 16, FEAT), bf16),
        in_specs=[ANY, ANY, ANY],
        out_specs=VM,
        scratch_shapes=[
            pltpu.VMEM((VIS, QDEV), i32),
            pltpu.VMEM((VIS * VIS, QDEV), i32),
            pltpu.SemaphoreType.DMA((3,)),
        ],
        compiler_params=PARAMS,
    )(in_hbm(tokens), in_hbm(owners), in_hbm(cands))


def build(blocks):
    return pl.pallas_call(
        build_kernel,
        out_shape=(
            jax.ShapeDtypeStruct((COLS, CELL, 16, FEAT), bf16),
            jax.ShapeDtypeStruct((QDEV * VIS, OWNERS), bf16),
            jax.ShapeDtypeStruct((QDEV * VIS, FEAT), f32),
        ),
        in_specs=[VM] * ROWS,
        out_specs=(VM, VM, VM),
        scratch_shapes=[
            pltpu.VMEM((ROWS * PIECES, 16, FEAT), bf16),
            pltpu.VMEM((8, COLS * QDEV), i32),
            pltpu.SMEM((8, COLS * QDEV), i32),
            pltpu.SemaphoreType.DMA,
        ],
        compiler_params=PARAMS,
    )(*blocks)


def score(got, passages, lengths):
    return pl.pallas_call(
        score_kernel,
        out_shape=jax.ShapeDtypeStruct((COLS, ROWS, 1, FEAT), f32),
        in_specs=[VM, VM, ANY, ANY],
        out_specs=VM,
        scratch_shapes=[
            pltpu.VMEM((LOCAL, PLEN, FEAT), bf16),
            pltpu.SMEM((LOCAL,), i32),
            pltpu.VMEM((16, TILES), i32),
            pltpu.SMEM((16, TILES), i32),
            pltpu.VMEM((TILES, SLOTS), f32),
            pltpu.SemaphoreType.DMA((3,)),
        ],
        compiler_params=PARAMS,
    )(got.reshape(COLS * CELL, 16, FEAT), got, in_hbm(passages), in_hbm(lengths))


def hand_back(pick, mask, got):
    return pl.pallas_call(
        return_kernel,
        out_shape=jax.ShapeDtypeStruct((QDEV, VIS * VIS), f32),
        in_specs=[VM, VM, VM],
        out_specs=VM,
        compiler_params=PARAMS,
    )(pick, mask, got)


def shards(query_tokens, visit_owner, visit_passages, passage_tokens, passage_lengths):
    own = pack(
        query_tokens.reshape(TOK, 16, FEAT),
        visit_owner.T,
        jnp.transpose(visit_passages, (1, 2, 0)).reshape(VIS * VIS, QDEV),
    )
    up = [(i, (i + 1) % ROWS) for i in range(ROWS)]
    down = [(i, (i + ROWS - 1) % ROWS) for i in range(ROWS)]
    blocks = [own]
    left = right = own
    for step in range(1, ROWS // 2):
        left = lax.ppermute(left, "qbatch", up)
        right = lax.ppermute(right, "qbatch", down)
        if step == 1:
            right, again = lax.optimization_barrier((right, own))
            far = lax.ppermute(again, "qbatch", [(i, (i + ROWS // 2) % ROWS) for i in range(ROWS)])
        blocks += [left, right]
    blocks.append(far)
    send, pick, mask = build(blocks)
    got = lax.all_to_all(send, "corpus", split_axis=0, concat_axis=0, tiled=True)
    scored = score(got, passage_tokens, passage_lengths)
    returned = lax.all_to_all(
        scored.reshape(OWNERS, 1, FEAT), ("corpus", "qbatch"), split_axis=0, concat_axis=0, tiled=True
    )
    return hand_back(pick, mask, returned.reshape(OWNERS, FEAT))


def solution(mesh):
    placed = (
        P(("corpus", "qbatch"), None, None),
        P(("corpus", "qbatch"), None),
        P(("corpus", "qbatch"), None, None),
        P(("corpus", "qbatch"), None, None),
        P(("corpus", "qbatch")),
    )
    return jax.shard_map(
        shards, mesh=mesh, in_specs=placed, out_specs=P(("corpus", "qbatch"), None), check_vma=False
    )
```

```python
import jax
import jax.numpy as jnp
from jax import lax
from jax.experimental import pallas as pl
from jax.experimental.pallas import tpu as pltpu
from jax.sharding import PartitionSpec as P

f32, bf16, i32 = jnp.float32, jnp.bfloat16, jnp.int32
TOK = 32
FEAT = 128
PLEN = 128
LOCAL = 64
VIS = 8
QDEV = 16
ROWS = 8
COLS = 32
GROUP = QDEV * ROWS
OWNERS = COLS * ROWS
SLOTS = COLS * VIS
PIECES = TOK + 1
CELL = VIS * 2 + 1
TILE = 8
TILES = 384
UNROLL = 96
VMEM_LIMIT = 16 * 1024 * 1024


def iota(shape, dim):
    return lax.broadcasted_iota(i32, shape, dim)


def dot_t(a, b, precision=None):
    return lax.dot_general(
        a, b, (((1,), (1,)), ((), ())), precision=precision, preferred_element_type=f32
    )


def dot_n(a, b, precision=None):
    return lax.dot_general(
        a, b, (((1,), (0,)), ((), ())), precision=precision, preferred_element_type=f32
    )


def dot_tn(a, b, precision=None):
    return lax.dot_general(
        a, b, (((0,), (0,)), ((), ())), precision=precision, preferred_element_type=f32
    )


def pack_kernel(tokens_ref, owner_ref, cand_ref, out_ref, owners, cands, sems):
    loads = [
        pltpu.make_async_copy(owner_ref, owners, sems.at[0]),
        pltpu.make_async_copy(cand_ref, cands, sems.at[1]),
        pltpu.make_async_copy(tokens_ref, out_ref.at[pl.ds(0, TOK)], sems.at[2]),
    ]
    for load in loads:
        load.start()
    loads[0].wait()
    loads[1].wait()
    rest = jnp.zeros((FEAT - VIS - VIS * VIS, QDEV), i32)
    lists = jnp.concatenate([owners[...] + 1, cands[...] + 1, rest], 0).astype(bf16)
    eye = (iota((FEAT, FEAT), 0) == iota((FEAT, FEAT), 1)).astype(bf16)
    out_ref[TOK] = dot_tn(lists, eye).astype(bf16)
    loads[2].wait()


def build_kernel(*refs):
    blocks = refs[:ROWS]
    send_ref, pick_ref, mask_ref, buf, idx_v, idx_s, idx_sem = refs[ROWS:]
    row = lax.axis_index("qbatch").astype(i32)
    lists = [
        jnp.where(lax.rem(row + step, ROWS) == z, block[TOK].astype(f32), 0.0)
        for z in range(ROWS)
        for block, step in zip(blocks, STEPS)
    ]
    lists = [sum(lists[z * ROWS : z * ROWS + ROWS]) for z in range(ROWS)]
    lists = jnp.concatenate(lists, 0).astype(bf16)
    eye = (iota((GROUP, FEAT), 0) == iota((GROUP, FEAT), 1)).astype(bf16)
    owners = dot_t(eye[0:QDEV], lists)
    wanted = (iota((COLS, GROUP), 0) * ROWS + (row + 1)).astype(f32)
    hit = jnp.zeros((COLS, GROUP), f32)
    for v in range(VIS):
        hit = jnp.where(owners[v : v + 1, :] == wanted, 1.0, hit)
    before = (iota((GROUP, GROUP), 0) < iota((GROUP, GROUP), 1)).astype(bf16)
    rank = dot_n(hit.astype(bf16), before)
    rank = jnp.where(hit > 0.5, rank, -1.0)
    place = iota((COLS, QDEV, GROUP), 1).astype(f32)
    pick = jnp.where(rank[:, None, :] == place, 1.0, 0.0)
    chosen = pick.reshape(COLS * QDEV, GROUP).astype(bf16)
    number = iota((QDEV, GROUP), 1).astype(bf16)
    query = dot_t(number, chosen)[0:8, :].astype(i32)
    idx_v[...] = (query >> 4) * PIECES + (query & (QDEV - 1)) * 2
    to_scalar = pltpu.make_async_copy(idx_v, idx_s, idx_sem)
    to_scalar.start()
    rows = dot_n(chosen, lists)
    lane = iota((COLS * QDEV, FEAT), 1)
    target = ((iota((COLS * QDEV, FEAT), 0) >> 4) * ROWS + (row + 1)).astype(f32)
    visit = jnp.where((rows == target) & (lane < VIS), 1.0, 0.0).astype(bf16)
    low, high = iota((FEAT, FEAT), 0), iota((FEAT, FEAT), 1)
    spread = ((high >= VIS) & (low == (high >> 3) - 1)).astype(bf16)
    kept = (rows * dot_n(visit, spread)).astype(bf16)
    send_ref[:, VIS * 2] = kept.reshape(COLS, QDEV, FEAT)
    every = (iota((GROUP, OWNERS), 1) + 1).astype(f32)
    theirs = lists.astype(f32)
    visited = jnp.zeros((GROUP, OWNERS), f32)
    for v in range(VIS):
        visited = jnp.where(theirs[:, v : v + 1] == every, 1.0, visited)
    earlier = (iota((QDEV, GROUP), 1) < iota((QDEV, GROUP), 0) + row * QDEV).astype(bf16)
    places = dot_n(earlier, visited.astype(bf16))
    ours = blocks[0][TOK].astype(f32)
    lane = iota((QDEV, FEAT), 1)
    for v in range(VIS):
        at = jnp.where(ours[:, v : v + 1] == every[0:QDEV], 1.0, 0.0)
        pick_ref[v * QDEV : (v + 1) * QDEV, :] = at.astype(bf16)
        place = jnp.sum(at * places, axis=1, keepdims=True).astype(i32)
        mask_ref[v * QDEV : (v + 1) * QDEV, :] = jnp.where((lane >> 3) == place, 1.0, 0.0)
    for block, step in zip(blocks, STEPS):
        buf[pl.ds(lax.rem(row + step, ROWS) * PIECES, PIECES)] = block[...]
    to_scalar.wait()

    def one(c, _):
        for s in range(VIS):
            send_ref[c, 2 * s : 2 * s + 2] = buf[pl.ds(idx_s[0, c * QDEV + s], 2)]
        return 0

    lax.fori_loop(0, COLS, one, 0)


def split3(x):
    high = x.astype(bf16)
    x = x - high.astype(f32)
    mid = x.astype(bf16)
    return high, mid, (x - mid.astype(f32)).astype(bf16)


def score_kernel(
    got, cells_ref, passage_ref, length_ref, out_ref, held, lengths, plan_v, plan_s, best, moves_v, sems
):
    load = pltpu.make_async_copy(passage_ref, held, sems.at[0])
    load.start()
    load_lengths = pltpu.make_async_copy(length_ref, lengths, sems.at[2])
    load_lengths.start()
    kept = cells_ref[:, VIS * 2].astype(f32)[:, 0:VIS, :].reshape(SLOTS, FEAT)
    low, high = iota((FEAT, FEAT), 0), iota((FEAT, FEAT), 1)
    k16, l16 = iota((16, FEAT), 0), iota((16, FEAT), 1)
    fold = ((l16 >= VIS) & (l16 < VIS + VIS * VIS) & ((l16 & 7) == k16)).astype(bf16)
    cands = dot_t(fold, kept.astype(bf16))

    wide = (LOCAL, SLOTS)
    passage = (iota(wide, 0) + 1).astype(f32)
    slot = iota(wide, 1)
    hit = jnp.zeros(wide, f32)
    for k in range(VIS):
        hit = jnp.where(cands[k : k + 1, :] == passage, 1.0, hit)
    hits = hit.astype(bf16)
    before = (iota((SLOTS, SLOTS), 0) < iota((SLOTS, SLOTS), 1)).astype(bf16)
    rank = dot_n(hits, before).astype(i32)
    count = jnp.sum(hit, axis=1, keepdims=True).astype(i32)
    tiles = (count + (TILE - 1)) >> 3
    tiles_wide = jnp.broadcast_to(tiles, (LOCAL, FEAT)).astype(bf16)
    earlier = (iota((LOCAL, LOCAL), 1) < iota((LOCAL, LOCAL), 0)).astype(bf16)
    first_wide = dot_n(earlier, tiles_wide).astype(i32)
    padded = jnp.concatenate([hits, jnp.zeros(wide, bf16)], 0)
    tiles_row = (dot_t(jnp.ones((16, SLOTS), bf16), padded).astype(i32) + (TILE - 1)) >> 3
    first_row = dot_n(tiles_row.astype(bf16), (low < high).astype(bf16)).astype(i32)
    total = first_row[0:1, FEAT - 1 : FEAT]

    shift = slot - rank
    x = jnp.where(hit > 0.5, shift * 512 + slot + 1, 0)
    for b in range(8):
        moves = ((x >> (9 + b)) & 1) == 1
        x = jnp.where(moves, 0, x) + pltpu.roll(jnp.where(moves, x, 0), SLOTS - (1 << b), 1)
    packed = jnp.maximum((x & 511) - 1, 0).astype(f32).astype(bf16)

    t = iota((TILES, FEAT), 0)
    own = (first_row[0:1] <= t) & (t < first_row[0:1] + tiles_row[0:1])
    own = jnp.where(own, 1.0, 0.0).astype(bf16)
    table = jnp.concatenate(
        [packed, (first_wide >> 4).astype(bf16), (first_wide & 15).astype(bf16)], 1
    )
    rows = dot_n(own[:, 0:LOCAL], table)
    begun = rows[:, SLOTS : SLOTS + FEAT].astype(i32) * 16
    depth = t - begun - rows[:, SLOTS + FEAT :].astype(i32)
    depth = jnp.concatenate([depth, depth], 1)
    here = ((iota((TILES, SLOTS), 1) >> 3) == depth) & (iota((TILES, SLOTS), 0) < total)
    chosen = jnp.where(here, rows[:, 0:SLOTS], 0.0).astype(bf16)
    k16, l16 = iota((16, SLOTS + FEAT), 0), iota((16, SLOTS + FEAT), 1)
    fold = jnp.where((l16 < SLOTS) & ((l16 & 7) == k16), 1.0, 0.0)
    fold = jnp.where((l16 >= SLOTS) & (k16 == TILE), (l16 - SLOTS).astype(f32), fold)
    plan = dot_t(fold.astype(bf16), jnp.concatenate([chosen, own], 1)).astype(i32)
    plan_v[0:TILE, :] = plan[0:TILE] * 2 + (plan[0:TILE] >> 3)
    plan_v[TILE : TILE + 1, :] = plan[TILE : TILE + 1]
    plan_v[TILE + 1 : TILE + 2, :] = jnp.broadcast_to(total, (1, TILES))
    to_scalar = pltpu.make_async_copy(plan_v, plan_s, sems.at[1])
    to_scalar.start()
    adder = ((iota((SLOTS, FEAT), 0) >> 5) == (iota((SLOTS, FEAT), 1) & 7)).astype(bf16)
    first = first_wide[:, 0:1]
    t = iota((LOCAL, TILES), 1)
    owned = jnp.where((first <= t) & (t < first + tiles), 1.0, 0.0).astype(bf16)
    x = x >> 9
    for b in (7, 6, 5, 4, 3, 2, 1, 0):
        moves = ((x >> b) & 1) == 1
        moves_v[b] = jnp.where(moves, 1.0, 0.0)
        x = jnp.where(moves, 0, x) + pltpu.roll(jnp.where(moves, x, 0), 1 << b, 1)
    to_scalar.wait()
    load_lengths.wait()
    load.wait()
    token = iota((PLEN, FEAT), 0)

    def tile_steps(step, _):
        for half in range(UNROLL // 8):
            found = []
            for u in range(8):
                t = step * UNROLL + half * 8 + u
                queries = jnp.concatenate(
                    [got[pl.ds(plan_s[r, t], 2)].reshape(TOK, FEAT) for r in range(TILE)], 0
                )
                p = plan_s[TILE, t]
                tokens = held[p].astype(f32)
                tokens = jnp.where(token < lengths[p], tokens, tokens[0:1, :]).astype(bf16)
                similarity = dot_t(tokens, queries)
                found.append(jnp.max(similarity, axis=0, keepdims=True))
            at = pl.multiple_of(step * UNROLL + half * 8, 8)
            best[pl.ds(at, 8), :] = jnp.concatenate(found, 0)
        return 0

    lax.fori_loop(0, (plan_s[TILE + 1, 0] + (UNROLL - 1)) // UNROLL, tile_steps, 0)

    sums = dot_n(jnp.concatenate(split3(best[...]), 1), jnp.concatenate([adder] * 3, 0))
    sums = jnp.where(here, jnp.concatenate([sums, sums], 1), 0.0)
    y = dot_n(jnp.concatenate([owned] * 3, 1), jnp.concatenate(split3(sums), 0))
    y = jnp.where(slot < count, y, 0.0)
    for b in (7, 6, 5, 4, 3, 2, 1, 0):
        moved = y * moves_v[b]
        y = (y - moved) + pltpu.roll(moved, 1 << b, 1)
    scores = jnp.concatenate(
        [
            jnp.sum(jnp.where(cands[k : k + 1, :] == passage, y, 0.0), axis=0, keepdims=True)
            for k in range(VIS)
        ],
        0,
    )
    k8, l8 = iota((VIS, FEAT), 0), iota((VIS, FEAT), 1)
    repeat = ((l8 & 7) == k8).astype(f32)
    by_slot = dot_tn(scores, repeat, lax.Precision.HIGHEST)
    lane = iota((SLOTS, FEAT), 1)
    by_slot = jnp.where((lane >> 3) == (iota((SLOTS, FEAT), 0) & 7), by_slot, 0.0)
    by_group = jnp.sum(by_slot.reshape(COLS, VIS, FEAT), axis=1, keepdims=True)
    out_ref[...] = jnp.broadcast_to(by_group[:, None], (COLS, ROWS, 1, FEAT))


def return_kernel(pick_ref, mask_ref, got_ref, out_ref):
    pick = pick_ref[...]
    found = dot_n(jnp.concatenate([pick] * 3, 1), jnp.concatenate(split3(got_ref[...]), 0))
    found = jnp.where(mask_ref[...] > 0.5, found, 0.0)
    for step in (8, 16, 32, 64):
        found = found + pltpu.roll(found, step, 1)
    shape = (QDEV * VIS, FEAT)
    found = jnp.where((iota(shape, 1) >> 3) == (iota(shape, 0) >> 4), found, 0.0)
    out_ref[...] = jnp.sum(found.reshape(VIS, QDEV, FEAT), axis=0)[:, 0 : VIS * VIS]


VM = pl.BlockSpec(memory_space=pltpu.VMEM)
ANY = pl.BlockSpec(memory_space=pl.ANY)
PARAMS = pltpu.CompilerParams(vmem_limit_bytes=VMEM_LIMIT)
STEPS = (0, 7, 1, 6, 2, 5, 3, 4)


def in_hbm(x):
    return pltpu.with_memory_space_constraint(x, pltpu.HBM)


def pack(tokens, owners, cands):
    return pl.pallas_call(
        pack_kernel,
        out_shape=jax.ShapeDtypeStruct((PIECES, 16, FEAT), bf16),
        in_specs=[ANY, ANY, ANY],
        out_specs=VM,
        scratch_shapes=[
            pltpu.VMEM((VIS, QDEV), i32),
            pltpu.VMEM((VIS * VIS, QDEV), i32),
            pltpu.SemaphoreType.DMA((3,)),
        ],
        compiler_params=PARAMS,
    )(in_hbm(tokens), in_hbm(owners), in_hbm(cands))


def build(blocks):
    return pl.pallas_call(
        build_kernel,
        out_shape=(
            jax.ShapeDtypeStruct((COLS, CELL, 16, FEAT), bf16),
            jax.ShapeDtypeStruct((QDEV * VIS, OWNERS), bf16),
            jax.ShapeDtypeStruct((QDEV * VIS, FEAT), f32),
        ),
        in_specs=[VM] * ROWS,
        out_specs=(VM, VM, VM),
        scratch_shapes=[
            pltpu.VMEM((ROWS * PIECES, 16, FEAT), bf16),
            pltpu.VMEM((8, COLS * QDEV), i32),
            pltpu.SMEM((8, COLS * QDEV), i32),
            pltpu.SemaphoreType.DMA,
        ],
        compiler_params=PARAMS,
    )(*blocks)


def score(got, passages, lengths):
    return pl.pallas_call(
        score_kernel,
        out_shape=jax.ShapeDtypeStruct((COLS, ROWS, 1, FEAT), f32),
        in_specs=[VM, VM, ANY, ANY],
        out_specs=VM,
        scratch_shapes=[
            pltpu.VMEM((LOCAL, PLEN, FEAT), bf16),
            pltpu.SMEM((LOCAL,), i32),
            pltpu.VMEM((16, TILES), i32),
            pltpu.SMEM((16, TILES), i32),
            pltpu.VMEM((TILES, SLOTS), f32),
            pltpu.VMEM((8, LOCAL, SLOTS), f32),
            pltpu.SemaphoreType.DMA((3,)),
        ],
        compiler_params=PARAMS,
    )(got.reshape(COLS * CELL, 16, FEAT), got, in_hbm(passages), in_hbm(lengths))


def hand_back(pick, mask, got):
    return pl.pallas_call(
        return_kernel,
        out_shape=jax.ShapeDtypeStruct((QDEV, VIS * VIS), f32),
        in_specs=[VM, VM, VM],
        out_specs=VM,
        compiler_params=PARAMS,
    )(pick, mask, got)


def shards(query_tokens, visit_owner, visit_passages, passage_tokens, passage_lengths):
    own = pack(
        query_tokens.reshape(TOK, 16, FEAT),
        visit_owner.T,
        jnp.transpose(visit_passages, (1, 2, 0)).reshape(VIS * VIS, QDEV),
    )
    up = [(i, (i + 1) % ROWS) for i in range(ROWS)]
    down = [(i, (i + ROWS - 1) % ROWS) for i in range(ROWS)]
    blocks = [own]
    left = right = own
    for step in range(1, ROWS // 2):
        left = lax.ppermute(left, "qbatch", up)
        right = lax.ppermute(right, "qbatch", down)
        if step == 1:
            right, again = lax.optimization_barrier((right, own))
            far = lax.ppermute(again, "qbatch", [(i, (i + ROWS // 2) % ROWS) for i in range(ROWS)])
        blocks += [left, right]
    blocks.append(far)
    send, pick, mask = build(blocks)
    got = lax.all_to_all(send, "corpus", split_axis=0, concat_axis=0, tiled=True)
    scored = score(got, passage_tokens, passage_lengths)
    returned = lax.all_to_all(
        scored.reshape(OWNERS, 1, FEAT), ("corpus", "qbatch"), split_axis=0, concat_axis=0, tiled=True
    )
    return hand_back(pick, mask, returned.reshape(OWNERS, FEAT))


def solution(mesh):
    placed = (
        P(("corpus", "qbatch"), None, None),
        P(("corpus", "qbatch"), None),
        P(("corpus", "qbatch"), None, None),
        P(("corpus", "qbatch"), None, None),
        P(("corpus", "qbatch")),
    )
    return jax.shard_map(
        shards, mesh=mesh, in_specs=placed, out_specs=P(("corpus", "qbatch"), None), check_vma=False
    )
```

```python
import jax
import jax.numpy as jnp
from jax import lax
from jax.experimental import pallas as pl
from jax.experimental.pallas import tpu as pltpu
from jax.sharding import PartitionSpec as P

f32, bf16, i32 = jnp.float32, jnp.bfloat16, jnp.int32
TOK = 32
FEAT = 128
PLEN = 128
LOCAL = 64
VIS = 8
QDEV = 16
ROWS = 8
COLS = 32
GROUP = QDEV * ROWS
OWNERS = COLS * ROWS
SLOTS = COLS * VIS
PIECES = TOK + 1
CELL = VIS * 2 + 1
TILE = 8
TILES = 384
UNROLL = 72
VMEM_LIMIT = 16 * 1024 * 1024


def iota(shape, dim):
    return lax.broadcasted_iota(i32, shape, dim)


def dot_t(a, b, precision=None):
    return lax.dot_general(
        a, b, (((1,), (1,)), ((), ())), precision=precision, preferred_element_type=f32
    )


def dot_n(a, b, precision=None):
    return lax.dot_general(
        a, b, (((1,), (0,)), ((), ())), precision=precision, preferred_element_type=f32
    )


def dot_tn(a, b, precision=None):
    return lax.dot_general(
        a, b, (((0,), (0,)), ((), ())), precision=precision, preferred_element_type=f32
    )


def pack_kernel(tokens_ref, owner_ref, cand_ref, out_ref, owners, cands, sems):
    loads = [
        pltpu.make_async_copy(owner_ref, owners, sems.at[0]),
        pltpu.make_async_copy(cand_ref, cands, sems.at[1]),
        pltpu.make_async_copy(tokens_ref, out_ref.at[pl.ds(0, TOK)], sems.at[2]),
    ]
    for load in loads:
        load.start()
    loads[0].wait()
    loads[1].wait()
    rest = jnp.zeros((FEAT - VIS - VIS * VIS, QDEV), i32)
    lists = jnp.concatenate([owners[...] + 1, cands[...] + 1, rest], 0).astype(bf16)
    eye = (iota((FEAT, FEAT), 0) == iota((FEAT, FEAT), 1)).astype(bf16)
    out_ref[TOK] = dot_tn(lists, eye).astype(bf16)
    loads[2].wait()


def build_kernel(*refs):
    blocks = refs[:ROWS]
    send_ref, pick_ref, mask_ref, buf, idx_v, idx_s, idx_sem = refs[ROWS:]
    row = lax.axis_index("qbatch").astype(i32)
    lists = [
        jnp.where(lax.rem(row + step, ROWS) == z, block[TOK].astype(f32), 0.0)
        for z in range(ROWS)
        for block, step in zip(blocks, STEPS)
    ]
    lists = [sum(lists[z * ROWS : z * ROWS + ROWS]) for z in range(ROWS)]
    lists = jnp.concatenate(lists, 0).astype(bf16)
    eye = (iota((GROUP, FEAT), 0) == iota((GROUP, FEAT), 1)).astype(bf16)
    owners = dot_t(eye[0:QDEV], lists)
    wanted = (iota((COLS, GROUP), 0) * ROWS + (row + 1)).astype(f32)
    hit = jnp.zeros((COLS, GROUP), f32)
    for v in range(VIS):
        hit = jnp.where(owners[v : v + 1, :] == wanted, 1.0, hit)
    before = (iota((GROUP, GROUP), 0) < iota((GROUP, GROUP), 1)).astype(bf16)
    rank = dot_n(hit.astype(bf16), before)
    rank = jnp.where(hit > 0.5, rank, -1.0)
    place = iota((COLS, QDEV, GROUP), 1).astype(f32)
    pick = jnp.where(rank[:, None, :] == place, 1.0, 0.0)
    chosen = pick.reshape(COLS * QDEV, GROUP).astype(bf16)
    number = iota((QDEV, GROUP), 1).astype(bf16)
    query = dot_t(number, chosen)[0:8, :].astype(i32)
    idx_v[...] = (query >> 4) * PIECES + (query & (QDEV - 1)) * 2
    to_scalar = pltpu.make_async_copy(idx_v, idx_s, idx_sem)
    to_scalar.start()
    rows = dot_n(chosen, lists)
    lane = iota((COLS * QDEV, FEAT), 1)
    target = ((iota((COLS * QDEV, FEAT), 0) >> 4) * ROWS + (row + 1)).astype(f32)
    visit = jnp.where((rows == target) & (lane < VIS), 1.0, 0.0).astype(bf16)
    low, high = iota((FEAT, FEAT), 0), iota((FEAT, FEAT), 1)
    spread = ((high >= VIS) & (low == (high >> 3) - 1)).astype(bf16)
    kept = (rows * dot_n(visit, spread)).astype(bf16)
    send_ref[:, VIS * 2] = kept.reshape(COLS, QDEV, FEAT)
    every = (iota((GROUP, OWNERS), 1) + 1).astype(f32)
    theirs = lists.astype(f32)
    visited = jnp.zeros((GROUP, OWNERS), f32)
    for v in range(VIS):
        visited = jnp.where(theirs[:, v : v + 1] == every, 1.0, visited)
    earlier = (iota((QDEV, GROUP), 1) < iota((QDEV, GROUP), 0) + row * QDEV).astype(bf16)
    places = dot_n(earlier, visited.astype(bf16))
    ours = blocks[0][TOK].astype(f32)
    lane = iota((QDEV, FEAT), 1)
    for v in range(VIS):
        at = jnp.where(ours[:, v : v + 1] == every[0:QDEV], 1.0, 0.0)
        pick_ref[v * QDEV : (v + 1) * QDEV, :] = at.astype(bf16)
        place = jnp.sum(at * places, axis=1, keepdims=True).astype(i32)
        mask_ref[v * QDEV : (v + 1) * QDEV, :] = jnp.where((lane >> 3) == place, 1.0, 0.0)
    for block, step in zip(blocks, STEPS):
        buf[pl.ds(lax.rem(row + step, ROWS) * PIECES, PIECES)] = block[...]
    to_scalar.wait()

    def one(c, _):
        for s in range(VIS):
            send_ref[c, 2 * s : 2 * s + 2] = buf[pl.ds(idx_s[0, c * QDEV + s], 2)]
        return 0

    lax.fori_loop(0, COLS, one, 0)


def split3(x):
    high = x.astype(bf16)
    x = x - high.astype(f32)
    mid = x.astype(bf16)
    return high, mid, (x - mid.astype(f32)).astype(bf16)


def score_kernel(
    got, cells_ref, passage_ref, length_ref, out_ref, held, lengths, plan_v, plan_s, best, moves_v, sems
):
    load = pltpu.make_async_copy(passage_ref, held, sems.at[0])
    load.start()
    load_lengths = pltpu.make_async_copy(length_ref, lengths, sems.at[2])
    load_lengths.start()
    kept = cells_ref[:, VIS * 2].astype(f32)[:, 0:VIS, :].reshape(SLOTS, FEAT)
    low, high = iota((FEAT, FEAT), 0), iota((FEAT, FEAT), 1)
    k16, l16 = iota((16, FEAT), 0), iota((16, FEAT), 1)
    fold = ((l16 >= VIS) & (l16 < VIS + VIS * VIS) & ((l16 & 7) == k16)).astype(bf16)
    cands = dot_t(fold, kept.astype(bf16))

    wide = (LOCAL, SLOTS)
    passage = (iota(wide, 0) + 1).astype(f32)
    slot = iota(wide, 1)
    hit = jnp.zeros(wide, f32)
    for k in range(VIS):
        hit = jnp.where(cands[k : k + 1, :] == passage, 1.0, hit)
    hits = hit.astype(bf16)
    before = (iota((SLOTS, SLOTS), 0) < iota((SLOTS, SLOTS), 1)).astype(bf16)
    rank = dot_n(hits, before).astype(i32)
    count = jnp.sum(hit, axis=1, keepdims=True).astype(i32)
    tiles = (count + (TILE - 1)) >> 3
    tiles_wide = jnp.broadcast_to(tiles, (LOCAL, FEAT)).astype(bf16)
    earlier = (iota((LOCAL, LOCAL), 1) < iota((LOCAL, LOCAL), 0)).astype(bf16)
    first_wide = dot_n(earlier, tiles_wide).astype(i32)
    padded = jnp.concatenate([hits, jnp.zeros(wide, bf16)], 0)
    tiles_row = (dot_t(jnp.ones((16, SLOTS), bf16), padded).astype(i32) + (TILE - 1)) >> 3
    first_row = dot_n(tiles_row.astype(bf16), (low < high).astype(bf16)).astype(i32)
    total = first_row[0:1, FEAT - 1 : FEAT]

    shift = slot - rank
    x = jnp.where(hit > 0.5, shift * 512 + slot + 1, 0)
    for b in range(8):
        moves = ((x >> (9 + b)) & 1) == 1
        x = jnp.where(moves, 0, x) + pltpu.roll(jnp.where(moves, x, 0), SLOTS - (1 << b), 1)
    packed = jnp.maximum((x & 511) - 1, 0).astype(f32).astype(bf16)

    t = iota((TILES, FEAT), 0)
    own = (first_row[0:1] <= t) & (t < first_row[0:1] + tiles_row[0:1])
    own = jnp.where(own, 1.0, 0.0).astype(bf16)
    table = jnp.concatenate(
        [packed, (first_wide >> 4).astype(bf16), (first_wide & 15).astype(bf16)], 1
    )
    rows = dot_n(own[:, 0:LOCAL], table)
    begun = rows[:, SLOTS : SLOTS + FEAT].astype(i32) * 16
    depth = t - begun - rows[:, SLOTS + FEAT :].astype(i32)
    depth = jnp.concatenate([depth, depth], 1)
    here = ((iota((TILES, SLOTS), 1) >> 3) == depth) & (iota((TILES, SLOTS), 0) < total)
    chosen = jnp.where(here, rows[:, 0:SLOTS], 0.0).astype(bf16)
    k16, l16 = iota((16, SLOTS + FEAT), 0), iota((16, SLOTS + FEAT), 1)
    fold = jnp.where((l16 < SLOTS) & ((l16 & 7) == k16), 1.0, 0.0)
    fold = jnp.where((l16 >= SLOTS) & (k16 == TILE), (l16 - SLOTS).astype(f32), fold)
    plan = dot_t(fold.astype(bf16), jnp.concatenate([chosen, own], 1)).astype(i32)
    plan_v[0:TILE, :] = plan[0:TILE] * 2 + (plan[0:TILE] >> 3)
    plan_v[TILE : TILE + 1, :] = plan[TILE : TILE + 1]
    plan_v[TILE + 1 : TILE + 2, :] = jnp.broadcast_to(total, (1, TILES))
    to_scalar = pltpu.make_async_copy(plan_v, plan_s, sems.at[1])
    to_scalar.start()
    adder = ((iota((SLOTS, FEAT), 0) >> 5) == (iota((SLOTS, FEAT), 1) & 7)).astype(bf16)
    first = first_wide[:, 0:1]
    t = iota((LOCAL, TILES), 1)
    owned = jnp.where((first <= t) & (t < first + tiles), 1.0, 0.0).astype(bf16)
    x = x >> 9
    for b in (7, 6, 5, 4, 3, 2, 1, 0):
        moves = ((x >> b) & 1) == 1
        moves_v[b] = jnp.where(moves, 1.0, 0.0)
        x = jnp.where(moves, 0, x) + pltpu.roll(jnp.where(moves, x, 0), 1 << b, 1)
    to_scalar.wait()
    load_lengths.wait()
    load.wait()
    token = iota((PLEN, FEAT), 0)

    def tile_steps(step, _):
        for half in range(UNROLL // 8):
            found = []
            for u in range(8):
                t = step * UNROLL + half * 8 + u
                queries = jnp.concatenate(
                    [got[pl.ds(plan_s[r, t], 2)].reshape(TOK, FEAT) for r in range(TILE)], 0
                )
                p = plan_s[TILE, t]
                tokens = held[p].astype(f32)
                tokens = jnp.where(token < lengths[p], tokens, tokens[0:1, :]).astype(bf16)
                similarity = dot_t(tokens, queries)
                found.append(jnp.max(similarity, axis=0, keepdims=True))
            at = pl.multiple_of(step * UNROLL + half * 8, 8)
            best[pl.ds(at, 8), :] = jnp.concatenate(found, 0)
        return 0

    lax.fori_loop(0, (plan_s[TILE + 1, 0] + (UNROLL - 1)) // UNROLL, tile_steps, 0)

    sums = dot_n(jnp.concatenate(split3(best[...]), 1), jnp.concatenate([adder] * 3, 0))
    sums = jnp.where(here, jnp.concatenate([sums, sums], 1), 0.0)
    y = dot_n(jnp.concatenate([owned] * 3, 1), jnp.concatenate(split3(sums), 0))
    y = jnp.where(slot < count, y, 0.0)
    for b in (7, 6, 5, 4, 3, 2, 1, 0):
        moved = y * moves_v[b]
        y = (y - moved) + pltpu.roll(moved, 1 << b, 1)
    scores = jnp.concatenate(
        [
            jnp.sum(jnp.where(cands[k : k + 1, :] == passage, y, 0.0), axis=0, keepdims=True)
            for k in range(VIS)
        ],
        0,
    )
    k8, l8 = iota((VIS, FEAT), 0), iota((VIS, FEAT), 1)
    repeat = ((l8 & 7) == k8).astype(f32)
    by_slot = dot_tn(scores, repeat, lax.Precision.HIGHEST)
    lane = iota((SLOTS, FEAT), 1)
    by_slot = jnp.where((lane >> 3) == (iota((SLOTS, FEAT), 0) & 7), by_slot, 0.0)
    by_group = jnp.sum(by_slot.reshape(COLS, VIS, FEAT), axis=1, keepdims=True)
    out_ref[...] = jnp.broadcast_to(by_group[:, None], (COLS, ROWS, 1, FEAT))


def return_kernel(pick_ref, mask_ref, got_ref, out_ref):
    pick = pick_ref[...]
    found = dot_n(jnp.concatenate([pick] * 3, 1), jnp.concatenate(split3(got_ref[...]), 0))
    found = jnp.where(mask_ref[...] > 0.5, found, 0.0)
    for step in (8, 16, 32, 64):
        found = found + pltpu.roll(found, step, 1)
    shape = (QDEV * VIS, FEAT)
    found = jnp.where((iota(shape, 1) >> 3) == (iota(shape, 0) >> 4), found, 0.0)
    out_ref[...] = jnp.sum(found.reshape(VIS, QDEV, FEAT), axis=0)[:, 0 : VIS * VIS]


VM = pl.BlockSpec(memory_space=pltpu.VMEM)
ANY = pl.BlockSpec(memory_space=pl.ANY)
PARAMS = pltpu.CompilerParams(vmem_limit_bytes=VMEM_LIMIT)
STEPS = (0, 7, 1, 6, 2, 5, 3, 4)


def in_hbm(x):
    return pltpu.with_memory_space_constraint(x, pltpu.HBM)


def pack(tokens, owners, cands):
    return pl.pallas_call(
        pack_kernel,
        out_shape=jax.ShapeDtypeStruct((PIECES, 16, FEAT), bf16),
        in_specs=[ANY, ANY, ANY],
        out_specs=VM,
        scratch_shapes=[
            pltpu.VMEM((VIS, QDEV), i32),
            pltpu.VMEM((VIS * VIS, QDEV), i32),
            pltpu.SemaphoreType.DMA((3,)),
        ],
        compiler_params=PARAMS,
    )(in_hbm(tokens), in_hbm(owners), in_hbm(cands))


def build(blocks):
    return pl.pallas_call(
        build_kernel,
        out_shape=(
            jax.ShapeDtypeStruct((COLS, CELL, 16, FEAT), bf16),
            jax.ShapeDtypeStruct((QDEV * VIS, OWNERS), bf16),
            jax.ShapeDtypeStruct((QDEV * VIS, FEAT), f32),
        ),
        in_specs=[VM] * ROWS,
        out_specs=(VM, VM, VM),
        scratch_shapes=[
            pltpu.VMEM((ROWS * PIECES, 16, FEAT), bf16),
            pltpu.VMEM((8, COLS * QDEV), i32),
            pltpu.SMEM((8, COLS * QDEV), i32),
            pltpu.SemaphoreType.DMA,
        ],
        compiler_params=PARAMS,
    )(*blocks)


def score(got, passages, lengths):
    return pl.pallas_call(
        score_kernel,
        out_shape=jax.ShapeDtypeStruct((COLS, ROWS, 1, FEAT), f32),
        in_specs=[VM, VM, ANY, ANY],
        out_specs=VM,
        scratch_shapes=[
            pltpu.VMEM((LOCAL, PLEN, FEAT), bf16),
            pltpu.SMEM((LOCAL,), i32),
            pltpu.VMEM((16, TILES), i32),
            pltpu.SMEM((16, TILES), i32),
            pltpu.VMEM((TILES, SLOTS), f32),
            pltpu.VMEM((8, LOCAL, SLOTS), f32),
            pltpu.SemaphoreType.DMA((3,)),
        ],
        compiler_params=PARAMS,
    )(got.reshape(COLS * CELL, 16, FEAT), got, in_hbm(passages), in_hbm(lengths))


def hand_back(pick, mask, got):
    return pl.pallas_call(
        return_kernel,
        out_shape=jax.ShapeDtypeStruct((QDEV, VIS * VIS), f32),
        in_specs=[VM, VM, VM],
        out_specs=VM,
        compiler_params=PARAMS,
    )(pick, mask, got)


def shards(query_tokens, visit_owner, visit_passages, passage_tokens, passage_lengths):
    own = pack(
        query_tokens.reshape(TOK, 16, FEAT),
        visit_owner.T,
        jnp.transpose(visit_passages, (1, 2, 0)).reshape(VIS * VIS, QDEV),
    )
    up = [(i, (i + 1) % ROWS) for i in range(ROWS)]
    down = [(i, (i + ROWS - 1) % ROWS) for i in range(ROWS)]
    blocks = [own]
    left = right = own
    for step in range(1, ROWS // 2):
        left = lax.ppermute(left, "qbatch", up)
        right = lax.ppermute(right, "qbatch", down)
        if step == 1:
            right, again = lax.optimization_barrier((right, own))
            far = lax.ppermute(again, "qbatch", [(i, (i + ROWS // 2) % ROWS) for i in range(ROWS)])
        blocks += [left, right]
    blocks.append(far)
    send, pick, mask = build(blocks)
    got = lax.all_to_all(send, "corpus", split_axis=0, concat_axis=0, tiled=True)
    scored = score(got, passage_tokens, passage_lengths)
    returned = lax.all_to_all(
        scored.reshape(OWNERS, 1, FEAT), ("corpus", "qbatch"), split_axis=0, concat_axis=0, tiled=True
    )
    return hand_back(pick, mask, returned.reshape(OWNERS, FEAT))


def solution(mesh):
    placed = (
        P(("corpus", "qbatch"), None, None),
        P(("corpus", "qbatch"), None),
        P(("corpus", "qbatch"), None, None),
        P(("corpus", "qbatch"), None, None),
        P(("corpus", "qbatch")),
    )
    return jax.shard_map(
        shards, mesh=mesh, in_specs=placed, out_specs=P(("corpus", "qbatch"), None), check_vma=False
    )
```
